256 devices in a mesh: ctx: 64 (over y, x_lo, z), grp: 4 (over x_hi, core).
Axes of the slice: x: 4 (x_hi: 2, x_lo: 2; x = x_hi * 2 + x_lo), y: 4, z: 8, core: 2. Of those that a mesh axis runs over, the one named last changes fastest.
Arguments:
- queries: bfloat16 [4096, 5120], P('ctx', 'grp')
- cache_codes: int32 [2, 8, 32768, 128], P(None, 'grp', 'ctx'), may hold values from 0 to 15
- cache_scales: float32 [2, 8, 4, 32768], P(None, 'grp', None, 'ctx'), may hold values from 0.03 to 0.3, as said below
- pattern: int32 [8, 64, 256], P('grp', None, 'ctx'), may hold values from 0 to 1, as said below
- out_weight: bfloat16 [5120, 5120], P('grp', 'ctx'), may hold values from -0.25 to 0.25
Outputs:
- mixed: bfloat16 [4096, 5120], P('ctx', 'grp')
The draws below stay inside these ranges and needn't reach their ends.
Inputs may be any that keep to these rules, and one draw needn't show every extreme that they name: `cache_scales`: positive scales. `pattern`: for every key-value head and query block, page 0 is kept.
All inputs are finite; a program needn't handle non-finite values.
Results may differ from the reference program's by a relative error of at most 0.014.
Values may be sent and summed in bfloat16 or wider, within the bound.
No kernel may reach another device: no remote copies, remote signals or barrier semaphores. Data moves between devices by JAX's collectives and lax.ppermute only.
A program may use at most 64 MiB of HBM per device.

```python
import math
import jax
import jax.numpy as jnp
from jax import lax

D = 5120
QHEADS = 40
KV_HEADS = 8
DH = 128
SGROUPS = 4
PAGE = 128
QB = 64
CTX_DEV = 512
N_CTX = 64


def cache_codes_all(base):
    key = jax.random.fold_in(base, 11)
    return jax.random.randint(key, (2, KV_HEADS, CTX_DEV * N_CTX, DH), 0, 16, dtype=jnp.int32)


def cache_scales_all(base):
    key = jax.random.fold_in(base, 12)
    unit = jax.random.uniform(key, (2, KV_HEADS, SGROUPS, CTX_DEV * N_CTX), jnp.float32)
    return 0.03 * jnp.exp(unit * math.log(10.0))


def draw_queries(key, part):
    key = jax.random.fold_in(key, 3)
    total_q = QB * N_CTX
    drawn = jax.random.normal(key, (total_q, QHEADS * DH), jnp.float32)
    return jnp.clip(drawn, -6.0, 6.0).astype(jnp.bfloat16)


def draw_cache_codes(key, part):
    base = key
    return cache_codes_all(base)


def draw_cache_scales(key, part):
    base = key
    return cache_scales_all(base)


def draw_pattern(key, part):
    key = jax.random.fold_in(key, 5)
    vertical_key, slash_key = jax.random.split(key)
    pages = CTX_DEV * N_CTX // PAGE
    reach = CTX_DEV // PAGE
    page_index = jnp.arange(pages, dtype=jnp.int32)
    threshold = 60 + 540 * (pages - page_index) // pages
    rolls = jax.random.randint(vertical_key, (KV_HEADS, 1, pages), 0, 1000, dtype=jnp.int32)
    vertical = rolls < threshold[None, None, :]
    diagonal = (CTX_DEV * N_CTX - QB * N_CTX + jnp.arange(N_CTX, dtype=jnp.int32) * QB) // PAGE
    distance = diagonal[:, None] - page_index[None, :]
    inside = (distance >= 0) & (distance < reach)
    offsets = jax.random.randint(slash_key, (KV_HEADS, reach), 0, 2, dtype=jnp.int32)
    offsets = offsets.at[:, 0].set(1)
    chosen = offsets[:, jnp.clip(distance, 0, reach - 1)] == 1
    keep = vertical | inside[None] & chosen | (page_index == 0)[None, None, :]
    return keep.astype(jnp.int32)


def strengthened(entries, key, source, target, blocks, factor):
    owner, partner = [(jnp.arange(entries.shape[axis_at]) // (entries.shape[axis_at] // blocks)).reshape([-1 if axis == axis_at else 1 for axis in range(entries.ndim)]) for axis_at in (source, target)]
    chosen = jax.random.permutation(key, blocks)[partner]
    strong = (owner == chosen) | (owner == (partner + blocks // 2) % blocks)
    return jnp.where(strong, factor * entries, entries)


def steps_of(stream_key, shape, pieces, smallest, largest):
    loudness, own = 1.0, jax.random.fold_in(stream_key, 6)
    for dim, blocks in pieces:
        heights = jnp.exp(jax.random.uniform(jax.random.fold_in(own, dim), (blocks,), jnp.float32, smallest / len(pieces), largest / len(pieces)))
        loudness = loudness * jnp.repeat(heights, shape[dim] // blocks).reshape([-1 if axis == dim else 1 for axis in range(len(shape))])
    return loudness


def bell_draw_with(key, shape, scale, limit, pieces, heavy, kind=jnp.bfloat16):
    entries = scale * jax.random.normal(key, shape, jnp.float32)
    if pieces:
        entries = entries * steps_of(key, shape, pieces, -0.22, 0.18)
    return jnp.clip(strengthened(entries, jax.random.fold_in(key, 3), *heavy), -limit, limit).astype(kind)


def setup_inputs(seed: int = 0) -> dict:
    streams_of = jax.random.split(jax.random.key(seed), 6)
    return {
        "queries": draw_queries(jax.random.fold_in(streams_of[5], 71), 0),
        "cache_codes": draw_cache_codes(jax.random.fold_in(streams_of[5], 71), 0),
        "cache_scales": draw_cache_scales(jax.random.fold_in(streams_of[5], 71), 0),
        "pattern": draw_pattern(jax.random.fold_in(streams_of[5], 71), 0),
        "out_weight": bell_draw_with(streams_of[4], (QHEADS * DH, D), (QHEADS * DH) ** -0.5, 0.25, ((0, 4), (1, 64)), (0, 1, 64, 4.0)),
    }


NEG_FILL = -1e+30

def hadamard(order):
    index = jnp.arange(order, dtype=jnp.int32)
    common = index[:, None] & index[None, :]
    parity = jnp.zeros((order, order), jnp.int32)
    for shift_bit in range(int(order).bit_length()):
        parity = parity ^ common >> shift_bit & 1
    return jnp.where(parity == 1, -1.0, 1.0).astype(jnp.float32)

def dequantize(codes, scales):
    width = codes.shape[-1]
    groups = scales.shape[1]
    spread = jnp.repeat(scales, width // groups, axis=1)
    spread = jnp.transpose(spread, (0, 2, 1))
    return ((codes.astype(jnp.float32) - 7.5) * spread).astype(jnp.bfloat16)

def reference(queries, cache_codes, cache_scales, pattern, out_weight):
    context = CTX_DEV * N_CTX
    total_q = QB * N_CTX
    per_group = QHEADS // KV_HEADS
    factor = 1.0 / math.sqrt(DH)
    table = hadamard(DH)
    rotated = jnp.einsum('qhd,de->hqe', queries.reshape(total_q, QHEADS, DH).astype(jnp.float32), table, precision=lax.Precision.HIGHEST)
    rotated = (rotated * factor).astype(jnp.bfloat16).reshape(KV_HEADS, per_group, total_q, DH)
    keys = dequantize(cache_codes[0], cache_scales[0])
    values = dequantize(cache_codes[1], cache_scales[1])
    key_pos = jnp.arange(context, dtype=jnp.int32)

    def one_block(item):
        head = (item // N_CTX).astype(jnp.int32)
        block = (item % N_CTX).astype(jnp.int32)
        start = (block * QB).astype(jnp.int32)
        query_rows = lax.dynamic_slice(rotated, (head, jnp.int32(0), start, jnp.int32(0)), (1, per_group, QB, DH))[0].astype(jnp.float32)
        head_keys = lax.dynamic_index_in_dim(keys, head, 0, keepdims=False).astype(jnp.float32)
        head_values = lax.dynamic_index_in_dim(values, head, 0, keepdims=False).astype(jnp.float32)
        scores = jnp.einsum('pqd,kd->pqk', query_rows, head_keys, precision=lax.Precision.HIGHEST) * factor
        head_pattern = lax.dynamic_index_in_dim(pattern, head, 0, keepdims=False)
        page_keep = lax.dynamic_index_in_dim(head_pattern, block, 0, keepdims=False)
        keep_cols = jnp.repeat(page_keep, PAGE)
        query_pos = context - total_q + start + jnp.arange(QB, dtype=jnp.int32)
        allowed = (keep_cols[None, :] == 1) & (key_pos[None, :] <= query_pos[:, None])
        scores = jnp.where(allowed[None], scores, NEG_FILL)
        top = lax.optimization_barrier(jnp.max(scores, axis=-1, keepdims=True))
        weights = jnp.where(allowed[None], jnp.exp(scores - top), 0.0)
        total = lax.optimization_barrier(jnp.sum(weights, axis=-1))
        rounded = lax.optimization_barrier(weights.astype(jnp.bfloat16)).astype(jnp.float32)
        weighted = jnp.einsum('pqk,kd->pqd', rounded, head_values, precision=lax.Precision.HIGHEST)
        attended = weighted / total[..., None]
        restored = jnp.einsum('pqd,de->qpe', attended, table, precision=lax.Precision.HIGHEST) * factor
        return restored.astype(jnp.bfloat16)
    blocks = lax.map(one_block, jnp.arange(KV_HEADS * N_CTX, dtype=jnp.int32))
    blocks = blocks.reshape(KV_HEADS, N_CTX, QB, per_group, DH)
    blocks = jnp.transpose(blocks, (1, 2, 0, 3, 4)).reshape(total_q, QHEADS * DH)
    return jnp.dot(blocks, out_weight, preferred_element_type=jnp.float32).astype(jnp.bfloat16)
```

```python
import functools
import math

import jax
import jax.numpy as jnp
from jax import lax
from jax.experimental import pallas as pl
from jax.experimental.pallas import tpu as pltpu
from jax.sharding import Mesh
from jax.sharding import PartitionSpec as P

NEG_FILL = -1e30
LOG2E = math.log2(math.e)
VMEM_LIMIT = 48 * 1024 * 1024

Y, X, Z = "y", "x_lo", "z"
PLANE = (Y, X)
GRP = ("x_hi", "core")


def hadamard(order):
    index = jnp.arange(order, dtype=jnp.int32)
    common = index[:, None] & index[None, :]
    parity = jnp.zeros((order, order), jnp.int32)
    for shift_bit in range(int(order).bit_length()):
        parity = parity ^ common >> shift_bit & 1
    return jnp.where(parity == 1, -1.0, 1.0).astype(jnp.float32)


def dequantize_kernel(codes_ref, scales_ref, tail_ref, out_ref):
    kinds, groups, length, width = codes_ref.shape
    parts = scales_ref.shape[2]
    for kind in range(kinds):
        for g in range(groups):
            scales = scales_ref[kind, g]
            spread = jnp.concatenate(
                [
                    jnp.broadcast_to(scales[i : i + 1], (width // parts, length))
                    for i in range(parts)
                ],
                axis=0,
            )
            values = (codes_ref[kind, g].astype(jnp.float32) - 7.5) * spread.T
            out_ref[pl.ds((kind * groups + g) * length, length), :] = values.astype(jnp.bfloat16)
    out_ref[pl.ds(kinds * groups * length, tail_ref.shape[0]), :] = tail_ref[...]


def dequantize(codes, scales, tail):
    kinds, groups, length, width = codes.shape
    rows = kinds * groups * length + tail.shape[0]
    return pl.pallas_call(
        dequantize_kernel,
        out_shape=jax.ShapeDtypeStruct((rows, width), jnp.bfloat16),
        compiler_params=pltpu.CompilerParams(vmem_limit_bytes=VMEM_LIMIT),
        name="dequantize",
    )(codes, scales, tail)


def rotate_kernel(queries_ref, table_ref, out_ref):
    copies, heads, _, width = out_ref.shape
    scale = LOG2E / width
    for h in range(heads):
        turned = jnp.dot(
            queries_ref[:, h * width : (h + 1) * width],
            table_ref[...],
            preferred_element_type=jnp.float32,
        )
        turned = (turned * scale).astype(jnp.bfloat16)
        for copy in range(copies):
            out_ref[copy, h] = turned


def rotate(queries, table, copies):
    rows, columns = queries.shape
    width = table.shape[0]
    return pl.pallas_call(
        rotate_kernel,
        out_shape=jax.ShapeDtypeStruct((copies, columns // width, rows, width), jnp.bfloat16),
        compiler_params=pltpu.CompilerParams(vmem_limit_bytes=VMEM_LIMIT),
        name="rotate",
    )(queries, table)


def attend_kernel(shards, per_group, carried, last, reach_ref, q_ref, *refs):
    kv = refs[: 2 * shards]
    refs = refs[2 * shards :]
    if carried:
        o_in, lse_in = refs[:2]
        refs = refs[2:]
    blocks, _, rows, width = q_ref.shape
    tokens = rows // per_group
    g, tile = pl.program_id(0), pl.program_id(1)
    length = kv[0].shape[0]
    page = 128
    pages = length // page
    groups = pl.num_programs(0)
    all_blocks = blocks * pl.num_programs(1)
    ahead = lax.broadcasted_iota(jnp.int32, (tokens, page), 1) - lax.broadcasted_iota(
        jnp.int32, (tokens, page), 0
    )

    def block(i, _):
        q = q_ref[i, 0]
        parts = []
        for s in range(shards):
            scores = lax.dot_general(
                q, kv[2 * s][...], (((1,), (1,)), ((), ())), preferred_element_type=jnp.float32
            )
            for p in range(pages):
                reach = reach_ref[((s * groups + g) * all_blocks + tile * blocks + i) * pages + p]
                x = scores[:, p * page : (p + 1) * page].reshape(per_group, tokens, page)
                x = jnp.where((ahead <= reach)[None], x, NEG_FILL)
                parts.append(x.reshape(rows, page))
        top = functools.reduce(jnp.maximum, parts)
        top = jnp.max(top, axis=1, keepdims=True)
        if carried:
            lse = lse_in[i, 0]
            top = jnp.maximum(lse, top)
        else:
            top = jnp.broadcast_to(top, (rows, page))
        total = jnp.zeros((rows, page), jnp.float32)
        out = jnp.zeros((rows, width), jnp.float32)
        for s in range(shards):
            weights = [jnp.exp2(x - top) for x in parts[s * pages : (s + 1) * pages]]
            total = total + functools.reduce(jnp.add, weights)
            weights = jnp.concatenate([w.astype(jnp.bfloat16) for w in weights], axis=1)
            out = out + jnp.dot(weights, kv[2 * s + 1][...], preferred_element_type=jnp.float32)
        total = jnp.sum(total, axis=1, keepdims=True)
        if carried:
            kept = jnp.exp2(lse - top)
            total = total + kept
            out = out + kept * o_in[i, 0]
        out = out / total
        lse = top + jnp.log2(total)
        if not last:
            o_out, lse_out = refs
            o_out[i, 0] = out
            lse_out[i, 0] = lse
        else:
            (packed,) = refs
            packed[i, 0, pl.ds(0, rows), :] = out.astype(jnp.bfloat16)
            across = []
            for h in range(per_group):
                column = lse[h * tokens : (h + 1) * tokens]
                across.append(
                    jnp.sum(jnp.where(ahead == 0, column, 0.0), axis=0, keepdims=True)
                )
            across.append(jnp.zeros((8 - per_group, page), jnp.float32))
            across = jnp.concatenate(across, axis=0)
            high = across.astype(jnp.bfloat16).astype(jnp.float32)
            middle = (across - high).astype(jnp.bfloat16).astype(jnp.float32)
            low = across - high - middle
            tail = jnp.concatenate([high, middle, low, jnp.zeros_like(low)], axis=0)
            packed[i, 0, pl.ds(rows, 32), :] = tail.astype(jnp.bfloat16)
        return 0

    lax.fori_loop(0, blocks, block, 0, unroll=2)


def attend(q, shards, reach, carry, per_group, last):
    all_blocks, groups, rows, width = q.shape
    length = 512
    n = 4
    tiles = all_blocks // n

    def per_block(height):
        return pl.BlockSpec((n, 1, height, width), lambda g, t, reach: (t, g, 0, 0))

    in_specs = [per_block(rows)]
    operands = [q]
    for (keys, k_at), (values, v_at) in shards:
        in_specs.append(pl.BlockSpec((length, width), lambda g, t, reach, k_at=k_at: (k_at + g, 0)))
        in_specs.append(pl.BlockSpec((length, width), lambda g, t, reach, v_at=v_at: (v_at + g, 0)))
        operands += [keys, values]
    if carry is not None:
        in_specs += [per_block(rows), per_block(rows)]
        operands += list(carry)
    if last:
        out_shape = jax.ShapeDtypeStruct((all_blocks, groups, rows + 32, width), jnp.bfloat16)
        out_specs = per_block(rows + 32)
    else:
        out_shape = [jax.ShapeDtypeStruct((all_blocks, groups, rows, width), jnp.float32)] * 2
        out_specs = [per_block(rows)] * 2
    scores = all_blocks * groups * rows * length * len(shards)
    return pl.pallas_call(
        functools.partial(attend_kernel, len(shards), per_group, carry is not None, last),
        grid_spec=pltpu.PrefetchScalarGridSpec(
            num_scalar_prefetch=1,
            grid=(groups, tiles),
            in_specs=in_specs,
            out_specs=out_specs,
        ),
        out_shape=out_shape,
        compiler_params=pltpu.CompilerParams(vmem_limit_bytes=VMEM_LIMIT),
        cost_estimate=pl.CostEstimate(
            flops=8 * scores * width, bytes_accessed=8 * 1024 * 1024, transcendentals=scores
        ),
        name="attend",
    )(reach, *operands)


def combine_kernel(per_group, packed_ref, table_ref, out_ref):
    sources, _, height, width = packed_ref.shape
    rows = height - 32
    tokens = rows // per_group
    tail = packed_ref[:, 0, pl.ds(rows, 32), :].astype(jnp.float32)
    lse = tail[:, 0:8] + tail[:, 8:16] + tail[:, 16:24]
    weights = jnp.exp2(lse - jnp.max(lse, axis=0, keepdims=True))
    weights = weights / jnp.sum(weights, axis=0, keepdims=True)
    weights = weights.reshape(sources * 8, width).T
    for h in range(per_group):
        attended = jnp.zeros((tokens, width), jnp.float32)
        for e in range(sources):
            part = packed_ref[e, 0, pl.ds(h * tokens, tokens), :].astype(jnp.float32)
            attended = attended + part * weights[:tokens, e * 8 + h : e * 8 + h + 1]
        restored = jnp.dot(
            attended,
            table_ref[...],
            preferred_element_type=jnp.float32,
            precision=lax.Precision.HIGHEST,
        )
        restored = (restored * (1.0 / math.sqrt(width))).astype(jnp.bfloat16)
        for copy in range(out_ref.shape[0]):
            out_ref[copy, :, h * width : (h + 1) * width] = restored


def combine(packed, table, per_group, copies):
    sources, groups, height, width = packed.shape
    tokens = (height - 32) // per_group
    return pl.pallas_call(
        functools.partial(combine_kernel, per_group),
        grid=(groups,),
        in_specs=[
            pl.BlockSpec((sources, 1, height, width), lambda g: (0, g, 0, 0)),
            pl.BlockSpec((width, width), lambda g: (0, 0)),
        ],
        out_specs=pl.BlockSpec((copies, tokens, per_group * width), lambda g: (0, 0, g)),
        out_shape=jax.ShapeDtypeStruct((copies, tokens, groups * per_group * width), jnp.bfloat16),
        compiler_params=pltpu.CompilerParams(vmem_limit_bytes=VMEM_LIMIT),
        name="combine",
    )(packed, table)


def on_device(queries, cache_codes, cache_scales, pattern, out_weight):
    ny, nx, nz = (lax.axis_size(a) for a in (Y, X, Z))
    y, x, z = (lax.axis_index(a) for a in (Y, X, Z))
    plane = ny * nx
    block_rows = queries.shape[0]
    _, groups, shard_len, width = cache_codes.shape
    heads = queries.shape[1] // width
    per_group = heads // groups
    pages = pattern.shape[2]
    page = shard_len // pages
    blocks = pattern.shape[1]
    total_len = shard_len * blocks
    total_q = block_rows * blocks
    table = hadamard(width)

    weight_rows = lax.all_gather(out_weight.T, Z, axis=0, tiled=True)

    tail = pattern.reshape(-1, width).astype(jnp.bfloat16)
    marks = tail.shape[0]
    tail = jnp.concatenate([tail, jnp.zeros((16 - marks, width), jnp.bfloat16)], axis=0)
    own = dequantize(cache_codes, cache_scales, tail)
    cut = groups * shard_len

    def moved(block, step):
        return lax.ppermute(block, Z, [(i, (i + step) % nz) for i in range(nz)])

    rotated = rotate(queries, table.astype(jnp.bfloat16), plane)
    gathered = lax.all_to_all(rotated, PLANE, 0, 0)
    q = gathered.reshape(plane, groups, per_group * block_rows, width)

    block_at = jnp.arange(plane, dtype=jnp.int32) * nz + z
    first_query = total_len - total_q + block_at * block_rows

    def reach_of(rows, distance):
        shard = (y * nx + x) * nz + (z - distance) % nz
        kept = rows.astype(jnp.float32).reshape(groups, plane, nz, pages)
        kept = lax.dynamic_index_in_dim(kept, z, 2, keepdims=False)
        first_key = shard * shard_len + jnp.arange(pages, dtype=jnp.int32) * page
        causal = first_query[:, None] - first_key[None, :]
        causal = jnp.clip(causal, -2 * page, 2 * page)
        return jnp.where(kept > 0.5, causal[None], -2 * page).reshape(-1)

    def whole(block):
        return ((block, 0), (block, groups))

    def marks_of(block):
        return block[2 * cut : 2 * cut + marks]

    ahead, behind = own, own
    carry = None
    for distance in range(1, nz // 2):
        ahead, behind = moved(ahead, 1), moved(behind, -1)
        shards = [whole(ahead), whole(behind)]
        reach = [reach_of(marks_of(ahead), distance), reach_of(marks_of(behind), -distance)]
        if carry is None:
            shards = [whole(own)] + shards
            reach = [reach_of(marks_of(own), 0)] + reach
        carry = attend(q, shards, jnp.concatenate(reach), carry, per_group, False)
    far_keys, far_values = moved(ahead[:cut], 1), moved(behind[cut:], -1)
    reach = reach_of(far_values[cut : cut + marks], nz // 2)
    packed = attend(q, [((far_keys, 0), (far_values, 0))], reach, carry, per_group, True)

    received = lax.all_to_all(packed, PLANE, 0, 0)
    restored = combine(received, table, per_group, plane)
    restored = lax.all_to_all(restored, PLANE, 0, 0)
    terms = lax.dot_general(
        restored.reshape(plane * block_rows, heads * width),
        weight_rows,
        (((1,), (1,)), ((), ())),
        preferred_element_type=jnp.float32,
    ).astype(jnp.bfloat16)
    columns = terms.shape[1]
    terms = lax.all_to_all(terms.reshape(ny, nx, block_rows, columns), GRP, 0, 0)
    share = jnp.sum(terms.astype(jnp.float32), axis=0).astype(jnp.bfloat16)

    same = lax.dynamic_index_in_dim(share, x, 0, keepdims=False)
    other = lax.dynamic_index_in_dim(share, 1 - x, 0, keepdims=False)
    where = [(a, b, c) for a in range(ny) for b in range(nx) for c in range(ny)]

    def flat(a, b, c):
        return (a * nx + b) * ny + c

    same = lax.ppermute(
        same, (Y, X) + GRP, [(flat(a, b, c), flat(c, b, a)) for a, b, c in where]
    )
    other = lax.ppermute(
        other, (Y, X) + GRP, [(flat(a, b, c), flat(c, 1 - b, a)) for a, b, c in where]
    )
    left = jnp.where(x == 0, same, other)
    right = jnp.where(x == 0, other, same)
    return jnp.concatenate([left, right], axis=1)


def solution(mesh):
    parts = Mesh(mesh.devices.reshape(4, 2, 8, 2, 2), (Y, X, Z) + GRP)
    ctx = (Y, X, Z)
    placed = (
        P(ctx, GRP),
        P(None, GRP, ctx, None),
        P(None, GRP, None, ctx),
        P(GRP, None, ctx),
        P(GRP, ctx),
    )
    return jax.shard_map(
        on_device, mesh=parts, in_specs=placed, out_specs=P(ctx, GRP), check_vma=False
    )
```

```python
import functools
import math

import jax
import jax.numpy as jnp
from jax import lax
from jax.experimental import pallas as pl
from jax.experimental.pallas import tpu as pltpu
from jax.sharding import Mesh
from jax.sharding import PartitionSpec as P

NEG_FILL = -1e30
LOG2E = math.log2(math.e)
VMEM_LIMIT = 58 * 1024 * 1024

Y, X, Z = "y", "x_lo", "z"
PLANE = (Y, X)
GRP = ("x_hi", "core")


def hadamard(order):
    index = jnp.arange(order, dtype=jnp.int32)
    common = index[:, None] & index[None, :]
    parity = jnp.zeros((order, order), jnp.int32)
    for shift_bit in range(int(order).bit_length()):
        parity = parity ^ common >> shift_bit & 1
    return jnp.where(parity == 1, -1.0, 1.0).astype(jnp.float32)


def dequantize_kernel(codes_ref, scales_ref, marks_ref, *outs):
    kinds, groups, length, width = codes_ref.shape
    parts = scales_ref.shape[2]
    for g in range(groups):
        out = outs[g]
        for kind in range(kinds):
            scales = scales_ref[kind, g]
            spread = jnp.concatenate(
                [
                    jnp.broadcast_to(scales[i : i + 1], (width // parts, length))
                    for i in range(parts)
                ],
                axis=0,
            )
            values = (codes_ref[kind, g].astype(jnp.float32) - 7.5) * spread.T
            values = values.astype(jnp.bfloat16)
            for copy in range(out.shape[0]):
                out[copy, pl.ds(kind * length, length), :] = values
        for copy in range(out.shape[0]):
            out[copy, pl.ds(kinds * length, 16), :] = marks_ref[g, copy]


def dequantize(codes, scales, marks):
    kinds, groups, length, width = codes.shape
    copies = marks.shape[1]
    out = jax.ShapeDtypeStruct((copies, kinds * length + 16, width), jnp.bfloat16)
    return pl.pallas_call(
        dequantize_kernel,
        out_shape=[out] * groups,
        compiler_params=pltpu.CompilerParams(vmem_limit_bytes=VMEM_LIMIT),
        name="dequantize",
    )(codes, scales, marks)


def rotate_kernel(queries_ref, table_ref, out_ref):
    groups, rows, width = out_ref.shape
    tokens = queries_ref.shape[0]
    per_group = rows // tokens
    scale = LOG2E / width
    for h in range(groups * per_group):
        turned = jnp.dot(
            queries_ref[:, h * width : (h + 1) * width],
            table_ref[...],
            preferred_element_type=jnp.float32,
        )
        at = pl.ds(h % per_group * tokens, tokens)
        out_ref[h // per_group, at, :] = (turned * scale).astype(jnp.bfloat16)


def rotate(queries, table, groups):
    tokens, columns = queries.shape
    width = table.shape[0]
    rows = columns // width // groups * tokens
    return pl.pallas_call(
        rotate_kernel,
        out_shape=jax.ShapeDtypeStruct((groups, rows, width), jnp.bfloat16),
        compiler_params=pltpu.CompilerParams(vmem_limit_bytes=VMEM_LIMIT),
        name="rotate",
    )(queries, table)


def attend_kernel(per_group, unit, page, blocks, ordered, *refs):
    if ordered:
        reach_ref, order_ref = refs[:2]
        refs = refs[2:]
    else:
        reach_ref = refs[0]
        refs = refs[1:]
    q_refs, kv_ref, refs = refs[:blocks], refs[blocks], refs[blocks + 1 :]
    outs, (pages_ref, s_ref, top_ref, sum_ref, acc_ref) = refs[:-5], refs[-5:]
    _, rows, width = q_refs[0].shape
    tokens = rows // per_group
    sources, height, _ = kv_ref.shape
    length = (height - 16) // 2
    shard_pages = length // page
    all_pages = sources * shard_pages
    masked_at = all_pages + unit

    def place(p, counts):
        full, some = counts
        reaches = [reach_ref[p * blocks + b] for b in range(blocks)]
        low = functools.reduce(jnp.minimum, reaches)
        high = functools.reduce(jnp.maximum, reaches)
        pages_ref[full] = p
        pages_ref[masked_at + some] = p
        whole = low >= page - 1
        part = jnp.logical_and(high > -tokens, low < page - 1)
        return full + whole.astype(jnp.int32), some + part.astype(jnp.int32)

    start = (jnp.int32(0), jnp.int32(0))
    full, some = lax.fori_loop(0, all_pages, place, start, unroll=4)
    whole = full // unit

    def leftover(i, some):
        pages_ref[masked_at + some] = pages_ref[whole * unit + i]
        return some + 1

    some = lax.fori_loop(0, full - whole * unit, leftover, some)
    rounds = (some + unit - 1) // unit

    def pad(i, _):
        pages_ref[masked_at + some + i] = -1
        return 0

    lax.fori_loop(0, rounds * unit - some, pad, 0)

    ahead = lax.broadcasted_iota(jnp.int32, (tokens, page), 1) - lax.broadcasted_iota(
        jnp.int32, (tokens, page), 0
    )
    top_ref[...] = jnp.full(top_ref.shape, NEG_FILL, jnp.float32)
    sum_ref[...] = jnp.zeros(sum_ref.shape, jnp.float32)
    acc_ref[...] = jnp.zeros(acc_ref.shape, jnp.float32)

    def fetch(p, at):
        first = pl.multiple_of(at + p % shard_pages * page, page)
        return kv_ref[p // shard_pages, pl.ds(first, page), :]

    def first_pass(i, base, slot, masked):
        ps = [pages_ref[base + i * unit + u] for u in range(unit)]
        held = [jnp.maximum(p, 0) for p in ps]
        k = jnp.concatenate([fetch(p, 0) for p in held], axis=0)
        for b in range(blocks):
            at = pl.ds(b * rows, rows)
            s = lax.dot_general(
                q_refs[b][0], k, (((1,), (1,)), ((), ())), preferred_element_type=jnp.float32
            )
            top = top_ref[at, :]
            for u in range(unit):
                x = s[:, u * page : (u + 1) * page]
                if masked:
                    reach = jnp.where(ps[u] < 0, -2 * page, reach_ref[held[u] * blocks + b])
                    x = x.reshape(per_group, tokens, page)
                    x = jnp.where((ahead <= reach)[None], x, NEG_FILL).reshape(rows, page)
                s_ref[slot, at, u * page : (u + 1) * page] = x
                top = jnp.maximum(top, x)
            top_ref[at, :] = top
        return 0

    def second_pass(i, base, slot):
        held = [jnp.maximum(pages_ref[base + i * unit + u], 0) for u in range(unit)]
        v = jnp.concatenate([fetch(p, length) for p in held], axis=0)
        for b in range(blocks):
            at = pl.ds(b * rows, rows)
            top = top_ref[at, :]
            weights = [
                jnp.exp2(s_ref[slot, at, u * page : (u + 1) * page] - top) for u in range(unit)
            ]
            sum_ref[at, :] = sum_ref[at, :] + functools.reduce(jnp.add, weights)
            weights = jnp.concatenate([w.astype(jnp.bfloat16) for w in weights], axis=1)
            acc_ref[at, :] = acc_ref[at, :] + jnp.dot(
                weights, v, preferred_element_type=jnp.float32
            )
        return 0

    lax.fori_loop(0, whole, lambda i, _: first_pass(i, 0, i, False), 0)
    lax.fori_loop(0, rounds, lambda i, _: first_pass(i, masked_at, whole + i, True), 0)
    for b in range(blocks):
        at = pl.ds(b * rows, rows)
        top = jnp.max(top_ref[at, :], axis=1, keepdims=True)
        top_ref[at, :] = jnp.broadcast_to(top, (rows, page))
    lax.fori_loop(0, whole, lambda i, _: second_pass(i, 0, i), 0)
    lax.fori_loop(0, rounds, lambda i, _: second_pass(i, masked_at, whole + i), 0)
    for b in range(blocks):
        at = pl.ds(b * rows, rows)
        total = jnp.sum(sum_ref[at, :], axis=1, keepdims=True)
        total = jnp.maximum(total, 1e-30)
        out = (acc_ref[at, :] / total).astype(jnp.bfloat16)
        lse = top_ref[at, :] + jnp.log2(total)
        across = [
            jnp.sum(
                jnp.where(ahead == 0, lse[h * tokens : (h + 1) * tokens], 0.0),
                axis=0,
                keepdims=True,
            )
            for h in range(per_group)
        ]
        across.append(jnp.zeros((8 - per_group, page), jnp.float32))
        across = jnp.concatenate(across, axis=0)
        high = across.astype(jnp.bfloat16).astype(jnp.float32)
        middle = (across - high).astype(jnp.bfloat16).astype(jnp.float32)
        low = across - high - middle
        tail = jnp.concatenate([high, middle, low, jnp.zeros_like(low)], axis=0)
        tail = tail.astype(jnp.bfloat16)
        if ordered:
            outs[0][order_ref[b], pl.ds(0, rows), :] = out
            outs[0][order_ref[b], pl.ds(rows, 32), :] = tail
        else:
            outs[b][pl.ds(0, rows), :] = out
            outs[b][pl.ds(rows, 32), :] = tail


def attend(q_blocks, kv, g, per_group, reach, order=None):
    blocks = len(q_blocks)
    _, rows, width = q_blocks[0].shape
    sources, height, _ = kv.shape
    page = 128
    pages = sources * ((height - 16) // 2 // page)
    unit = 4
    ordered = order is not None
    prefetched = (reach, order) if ordered else (reach,)
    part = (rows + 32, width)
    if ordered:
        out_shape = jax.ShapeDtypeStruct((blocks,) + part, jnp.bfloat16)
        out_specs = pl.BlockSpec((blocks,) + part, lambda t, *_: (0, 0, 0))
    else:
        out_shape = [jax.ShapeDtypeStruct(part, jnp.bfloat16)] * blocks
        out_specs = [pl.BlockSpec(part, lambda t, *_: (0, 0))] * blocks
    scores = blocks * rows * pages * page // 2
    once = pl.Buffered(1)
    return pl.pallas_call(
        functools.partial(attend_kernel, per_group, unit, page, blocks, ordered),
        grid_spec=pltpu.PrefetchScalarGridSpec(
            num_scalar_prefetch=len(prefetched),
            grid=(1,),
            in_specs=[
                pl.BlockSpec((1, rows, width), lambda t, *_: (g, 0, 0), pipeline_mode=once)
            ]
            * blocks
            + [pl.BlockSpec(kv.shape, lambda t, *_: (0, 0, 0), pipeline_mode=once)],
            out_specs=out_specs,
            scratch_shapes=[
                pltpu.SMEM((2 * (pages + unit),), jnp.int32),
                pltpu.VMEM((pages // unit + 1, blocks * rows, unit * page), jnp.float32),
                pltpu.VMEM((blocks * rows, page), jnp.float32),
                pltpu.VMEM((blocks * rows, page), jnp.float32),
                pltpu.VMEM((blocks * rows, width), jnp.float32),
            ],
        ),
        out_shape=out_shape,
        compiler_params=pltpu.CompilerParams(vmem_limit_bytes=VMEM_LIMIT),
        cost_estimate=pl.CostEstimate(
            flops=8 * scores * width, bytes_accessed=8 * 1024 * 1024, transcendentals=scores
        ),
        name="attend",
    )(*prefetched, *q_blocks, kv)


def combine_kernel(per_group, *refs):
    parts, table_ref, out_ref = refs[:-2], refs[-2], refs[-1]
    if len(parts) == 1:
        parts = [parts[0].at[e] for e in range(parts[0].shape[0])]
    height, width = parts[0].shape
    rows = height - 32
    tokens = rows // per_group
    lse = []
    for part in parts:
        tail = part[pl.ds(rows, 32), :].astype(jnp.float32)
        lse.append(tail[0:8] + tail[8:16] + tail[16:24])
    top = functools.reduce(jnp.maximum, lse)
    weights = [jnp.exp2(x - top) for x in lse]
    total = functools.reduce(jnp.add, weights)
    weights = jnp.concatenate([w / total for w in weights], axis=0).T
    for h in range(per_group):
        attended = jnp.zeros((tokens, width), jnp.float32)
        for e, part in enumerate(parts):
            value = part[pl.ds(h * tokens, tokens), :].astype(jnp.float32)
            attended = attended + value * weights[:tokens, e * 8 + h : e * 8 + h + 1]
        restored = jnp.dot(
            attended,
            table_ref[...],
            preferred_element_type=jnp.float32,
            precision=lax.Precision.HIGHEST,
        )
        restored = (restored * (1.0 / math.sqrt(width))).astype(jnp.bfloat16)
        for copy in range(out_ref.shape[0]):
            out_ref[copy, :, h * width : (h + 1) * width] = restored


def combine(parts, table, per_group, copies):
    height, width = parts[0].shape[-2:]
    tokens = (height - 32) // per_group
    return pl.pallas_call(
        functools.partial(combine_kernel, per_group),
        out_shape=jax.ShapeDtypeStruct((copies, tokens, per_group * width), jnp.bfloat16),
        compiler_params=pltpu.CompilerParams(vmem_limit_bytes=VMEM_LIMIT),
        name="combine",
    )(*parts, table)


def on_device(queries, cache_codes, cache_scales, pattern, out_weight):
    ny, nx, nz = (lax.axis_size(a) for a in (Y, X, Z))
    y, x, z = (lax.axis_index(a) for a in (Y, X, Z))
    plane = ny * nx
    block_rows = queries.shape[0]
    _, groups, shard_len, width = cache_codes.shape
    heads = queries.shape[1] // width
    per_group = heads // groups
    pages = pattern.shape[2]
    page = shard_len // pages
    blocks = pattern.shape[1]
    total_len = shard_len * blocks
    total_q = block_rows * blocks
    table = hadamard(width)

    marks = pattern.reshape(groups, plane, 1, nz * pages).astype(jnp.bfloat16)
    marks = jnp.pad(marks, ((0, 0), (0, 0), (0, 15), (0, width - nz * pages)))
    shards = dequantize(cache_codes, cache_scales, marks)
    gathered = [lax.all_to_all(shard, PLANE, 0, 0) for shard in shards]

    def moved(block, step):
        return lax.ppermute(block, Z, [(i, (i + step) % nz) for i in range(nz)])

    rotated = rotate(queries, table.astype(jnp.bfloat16), groups)
    q_blocks = [rotated] + [moved(rotated, i) for i in range(1, nz)]
    at = (z - jnp.arange(nz, dtype=jnp.int32)) % nz
    first_query = total_len - total_q + ((y * nx + x) * nz + at) * block_rows

    weight_rows, _ = lax.optimization_barrier((out_weight.T, q_blocks[-1]))
    weight_rows = lax.all_gather(weight_rows, Z, axis=0, tiled=True)

    def reach_of(kv):
        kept = kv[:, 2 * shard_len, : nz * pages].astype(jnp.float32).reshape(plane, nz, pages)
        kept = jnp.transpose(kept, (0, 2, 1))
        kept = jnp.flip(jnp.roll(kept, nz - 1 - z, axis=2), axis=2)
        shard = jnp.arange(plane, dtype=jnp.int32) * nz + z
        first_key = shard[:, None] * shard_len + jnp.arange(pages, dtype=jnp.int32) * page
        causal = jnp.clip(first_query[None, None, :] - first_key[:, :, None], -2 * page, 2 * page)
        return jnp.where(kept > 0.5, causal, -2 * page).reshape(-1)

    parts = attend(q_blocks, gathered[0], 0, per_group, reach_of(gathered[0]))
    received = [[parts[0]] + [moved(parts[i], -i) for i in range(1, nz)]]
    parts = attend(q_blocks, gathered[1], 1, per_group, reach_of(gathered[1]), at)
    received.append([lax.all_to_all(parts, Z, 0, 0)])
    restored = [combine(r, table, per_group, plane) for r in received]
    restored = jnp.concatenate(restored, axis=2)
    restored = lax.all_to_all(restored, PLANE, 0, 0)
    terms = lax.dot_general(
        restored.reshape(plane * block_rows, heads * width),
        weight_rows,
        (((1,), (1,)), ((), ())),
        preferred_element_type=jnp.float32,
    ).astype(jnp.bfloat16)
    columns = terms.shape[1]
    terms = lax.all_to_all(terms.reshape(ny, nx, block_rows, columns), GRP, 0, 0)
    share = jnp.sum(terms.astype(jnp.float32), axis=0).astype(jnp.bfloat16)

    same = lax.dynamic_index_in_dim(share, x, 0, keepdims=False)
    other = lax.dynamic_index_in_dim(share, 1 - x, 0, keepdims=False)
    where = [(a, b, c) for a in range(ny) for b in range(nx) for c in range(ny)]

    def flat(a, b, c):
        return (a * nx + b) * ny + c

    same = lax.ppermute(
        same, (Y, X) + GRP, [(flat(a, b, c), flat(c, b, a)) for a, b, c in where]
    )
    other = lax.ppermute(
        other, (Y, X) + GRP, [(flat(a, b, c), flat(c, 1 - b, a)) for a, b, c in where]
    )
    left = jnp.where(x == 0, same, other)
    right = jnp.where(x == 0, other, same)
    return jnp.concatenate([left, right], axis=1)


def solution(mesh):
    parts = Mesh(mesh.devices.reshape(4, 2, 8, 2, 2), (Y, X, Z) + GRP)
    ctx = (Y, X, Z)
    placed = (
        P(ctx, GRP),
        P(None, GRP, ctx, None),
        P(None, GRP, None, ctx),
        P(GRP, None, ctx),
        P(GRP, ctx),
    )
    return jax.shard_map(
        on_device, mesh=parts, in_specs=placed, out_specs=P(ctx, GRP), check_vma=False
    )
```

```python
import functools
import math

import jax
import jax.numpy as jnp
from jax import lax
from jax.experimental import pallas as pl
from jax.experimental.pallas import tpu as pltpu
from jax.sharding import Mesh
from jax.sharding import PartitionSpec as P

NEG_FILL = -1e30
LOG2E = math.log2(math.e)
VMEM_LIMIT = 58 * 1024 * 1024

Y, X, Z = "y", "x_lo", "z"
PLANE = (Y, X)
GRP = ("x_hi", "core")


def hadamard(order):
    index = jnp.arange(order, dtype=jnp.int32)
    common = index[:, None] & index[None, :]
    parity = jnp.zeros((order, order), jnp.int32)
    for shift_bit in range(int(order).bit_length()):
        parity = parity ^ common >> shift_bit & 1
    return jnp.where(parity == 1, -1.0, 1.0).astype(jnp.float32)


def dequantize_kernel(g, codes_ref, scales_ref, marks_ref, after_ref, out):
    kinds, _, length, width = codes_ref.shape
    parts = scales_ref.shape[2]
    for kind in range(kinds):
        scales = scales_ref[kind, g]
        spread = jnp.concatenate(
            [
                jnp.broadcast_to(scales[i : i + 1], (width // parts, length))
                for i in range(parts)
            ],
            axis=0,
        )
        values = (codes_ref[kind, 0].astype(jnp.float32) - 7.5) * spread.T
        values = values.astype(jnp.bfloat16)
        for copy in range(out.shape[0]):
            out[copy, pl.ds(kind * length, length), :] = values
    if g == 0:
        for copy in range(out.shape[0]):
            out[copy, pl.ds(kinds * length, 16), :] = marks_ref[copy]


def dequantize(g, codes, scales, marks, after):
    kinds, groups, length, width = codes.shape
    copies = marks.shape[0]
    height = kinds * length + (16 if g == 0 else 0)
    return pl.pallas_call(
        functools.partial(dequantize_kernel, g),
        grid=(1,),
        in_specs=[
            pl.BlockSpec((kinds, 1, length, width), lambda i: (0, g, 0, 0)),
            pl.BlockSpec(scales.shape, lambda i: (0, 0, 0, 0)),
            pl.BlockSpec(marks.shape, lambda i: (0, 0, 0)),
            pl.BlockSpec(memory_space=pl.ANY),
        ],
        out_specs=pl.BlockSpec((copies, height, width), lambda i: (0, 0, 0)),
        out_shape=jax.ShapeDtypeStruct((copies, height, width), jnp.bfloat16),
        compiler_params=pltpu.CompilerParams(vmem_limit_bytes=VMEM_LIMIT),
        name="dequantize",
    )(codes, scales, marks, after)


def pass_kernel(block_ref, after_ref, out_ref):
    out_ref[...] = block_ref[...]


def tie_kernel(block_ref, after_ref, out_ref):
    pass


def tied(block, after):
    anywhere = pl.BlockSpec(memory_space=pl.ANY)
    return pl.pallas_call(
        tie_kernel,
        in_specs=[anywhere, anywhere],
        out_specs=anywhere,
        out_shape=jax.ShapeDtypeStruct(block.shape, block.dtype),
        input_output_aliases={0: 0},
        name="tie",
    )(block, after)


def passed_after(block, after):
    return pl.pallas_call(
        pass_kernel,
        in_specs=[pl.BlockSpec(memory_space=pltpu.VMEM), pl.BlockSpec(memory_space=pl.ANY)],
        out_shape=jax.ShapeDtypeStruct(block.shape, block.dtype),
        name="pass",
    )(block, after)


def rotate_kernel(queries_ref, table_ref, out_ref):
    groups, rows, width = out_ref.shape
    tokens = queries_ref.shape[0]
    per_group = rows // tokens
    scale = LOG2E / width
    for h in range(groups * per_group):
        turned = jnp.dot(
            queries_ref[:, h * width : (h + 1) * width],
            table_ref[...],
            preferred_element_type=jnp.float32,
        )
        at = pl.ds(h % per_group * tokens, tokens)
        out_ref[h // per_group, at, :] = (turned * scale).astype(jnp.bfloat16)


def rotate(queries, table, groups):
    tokens, columns = queries.shape
    width = table.shape[0]
    rows = columns // width // groups * tokens
    return pl.pallas_call(
        rotate_kernel,
        out_shape=jax.ShapeDtypeStruct((groups, rows, width), jnp.bfloat16),
        compiler_params=pltpu.CompilerParams(vmem_limit_bytes=VMEM_LIMIT),
        name="rotate",
    )(queries, table)


def attend_kernel(
    per_group, unit, page, ordered, reach_ref, order_ref, q_ref, kv_ref, after_ref, *refs
):
    outs, (pages_ref, s_ref, top_ref, sum_ref, acc_ref) = refs[:-5], refs[-5:]
    blocks, _, rows, width = q_ref.shape
    tokens = rows // per_group
    sources, height, _ = kv_ref.shape
    length = height // 2 // page * page
    shard_pages = length // page
    all_pages = sources * shard_pages
    masked_at = all_pages + unit

    def place(p, counts):
        full, some = counts
        reaches = [reach_ref[p * blocks + b] for b in range(blocks)]
        low = functools.reduce(jnp.minimum, reaches)
        high = functools.reduce(jnp.maximum, reaches)
        pages_ref[full] = p
        pages_ref[masked_at + some] = p
        whole = low >= page - 1
        part = jnp.logical_and(high > -tokens, low < page - 1)
        return full + whole.astype(jnp.int32), some + part.astype(jnp.int32)

    start = (jnp.int32(0), jnp.int32(0))
    full, some = lax.fori_loop(0, all_pages, place, start, unroll=4)
    whole = full // unit

    def leftover(i, some):
        pages_ref[masked_at + some] = pages_ref[whole * unit + i]
        return some + 1

    some = lax.fori_loop(0, full - whole * unit, leftover, some)
    rounds = (some + unit - 1) // unit

    def pad(i, _):
        pages_ref[masked_at + some + i] = -1
        return 0

    lax.fori_loop(0, rounds * unit - some, pad, 0)

    ahead = lax.broadcasted_iota(jnp.int32, (tokens, page), 1) - lax.broadcasted_iota(
        jnp.int32, (tokens, page), 0
    )
    top_ref[...] = jnp.full(top_ref.shape, NEG_FILL, jnp.float32)
    sum_ref[...] = jnp.zeros(sum_ref.shape, jnp.float32)
    acc_ref[...] = jnp.zeros(acc_ref.shape, jnp.float32)

    def fetch(p, at):
        first = pl.multiple_of(at + p % shard_pages * page, page)
        return kv_ref[p // shard_pages, pl.ds(first, page), :]

    def first_pass(i, base, slot, masked):
        ps = [pages_ref[base + i * unit + u] for u in range(unit)]
        held = [jnp.maximum(p, 0) for p in ps]
        k = jnp.concatenate([fetch(p, 0) for p in held], axis=0)
        for b in range(blocks):
            at = pl.ds(b * rows, rows)
            s = lax.dot_general(
                q_ref[order_ref[b], 0], k, (((1,), (1,)), ((), ())), preferred_element_type=jnp.float32
            )
            top = top_ref[at, :]
            for u in range(unit):
                x = s[:, u * page : (u + 1) * page]
                if masked:
                    reach = jnp.where(ps[u] < 0, -2 * page, reach_ref[held[u] * blocks + b])
                    x = x.reshape(per_group, tokens, page)
                    x = jnp.where((ahead <= reach)[None], x, NEG_FILL).reshape(rows, page)
                s_ref[slot, at, u * page : (u + 1) * page] = x
                top = jnp.maximum(top, x)
            top_ref[at, :] = top
        return 0

    def second_pass(i, base, slot):
        held = [jnp.maximum(pages_ref[base + i * unit + u], 0) for u in range(unit)]
        v = jnp.concatenate([fetch(p, length) for p in held], axis=0)
        for b in range(blocks):
            at = pl.ds(b * rows, rows)
            top = top_ref[at, :]
            weights = [
                jnp.exp2(s_ref[slot, at, u * page : (u + 1) * page] - top) for u in range(unit)
            ]
            sum_ref[at, :] = sum_ref[at, :] + functools.reduce(jnp.add, weights)
            weights = jnp.concatenate([w.astype(jnp.bfloat16) for w in weights], axis=1)
            acc_ref[at, :] = acc_ref[at, :] + jnp.dot(
                weights, v, preferred_element_type=jnp.float32
            )
        return 0

    lax.fori_loop(0, whole, lambda i, _: first_pass(i, 0, i, False), 0)
    lax.fori_loop(0, rounds, lambda i, _: first_pass(i, masked_at, whole + i, True), 0)
    for b in range(blocks):
        at = pl.ds(b * rows, rows)
        top = jnp.max(top_ref[at, :], axis=1, keepdims=True)
        top_ref[at, :] = jnp.broadcast_to(top, (rows, page))
    lax.fori_loop(0, whole, lambda i, _: second_pass(i, 0, i), 0)
    lax.fori_loop(0, rounds, lambda i, _: second_pass(i, masked_at, whole + i), 0)
    for b in range(blocks):
        at = pl.ds(b * rows, rows)
        total = jnp.sum(sum_ref[at, :], axis=1, keepdims=True)
        total = jnp.maximum(total, 1e-30)
        out = (acc_ref[at, :] / total).astype(jnp.bfloat16)
        lse = top_ref[at, :] + jnp.log2(total)
        across = [
            jnp.sum(
                jnp.where(ahead == 0, lse[h * tokens : (h + 1) * tokens], 0.0),
                axis=0,
                keepdims=True,
            )
            for h in range(per_group)
        ]
        across.append(jnp.zeros((8 - per_group, page), jnp.float32))
        across = jnp.concatenate(across, axis=0)
        high = across.astype(jnp.bfloat16).astype(jnp.float32)
        middle = (across - high).astype(jnp.bfloat16).astype(jnp.float32)
        low = across - high - middle
        tail = jnp.concatenate([high, middle, low, jnp.zeros_like(low)], axis=0)
        tail = tail.astype(jnp.bfloat16)
        if ordered:
            outs[0][order_ref[b], pl.ds(0, rows), :] = out
            outs[0][order_ref[b], pl.ds(rows, 32), :] = tail
        else:
            outs[b][pl.ds(0, rows), :] = out
            outs[b][pl.ds(rows, 32), :] = tail


def attend(q, kv, g, per_group, reach, order, ordered, after):
    blocks, _, rows, width = q.shape
    sources, height, _ = kv.shape
    page = 128
    pages = sources * (height // 2 // page)
    unit = 4
    part = (rows + 32, width)
    if ordered:
        out_shape = jax.ShapeDtypeStruct((blocks,) + part, jnp.bfloat16)
        out_specs = pl.BlockSpec((blocks,) + part, lambda t, *_: (0, 0, 0))
    else:
        out_shape = [jax.ShapeDtypeStruct(part, jnp.bfloat16)] * blocks
        out_specs = [pl.BlockSpec(part, lambda t, *_: (0, 0))] * blocks
    scores = blocks * rows * pages * page // 2
    once = pl.Buffered(1)
    return pl.pallas_call(
        functools.partial(attend_kernel, per_group, unit, page, ordered),
        grid_spec=pltpu.PrefetchScalarGridSpec(
            num_scalar_prefetch=2,
            grid=(1,),
            in_specs=[
                pl.BlockSpec(
                    (blocks, 1, rows, width), lambda t, *_: (0, g, 0, 0), pipeline_mode=once
                ),
                pl.BlockSpec(kv.shape, lambda t, *_: (0, 0, 0), pipeline_mode=once),
                pl.BlockSpec(memory_space=pl.ANY),
            ],
            out_specs=out_specs,
            scratch_shapes=[
                pltpu.SMEM((2 * (pages + unit),), jnp.int32),
                pltpu.VMEM((pages // unit + 1, blocks * rows, unit * page), jnp.float32),
                pltpu.VMEM((blocks * rows, page), jnp.float32),
                pltpu.VMEM((blocks * rows, page), jnp.float32),
                pltpu.VMEM((blocks * rows, width), jnp.float32),
            ],
        ),
        out_shape=out_shape,
        compiler_params=pltpu.CompilerParams(vmem_limit_bytes=VMEM_LIMIT),
        cost_estimate=pl.CostEstimate(
            flops=8 * scores * width, bytes_accessed=8 * 1024 * 1024, transcendentals=scores
        ),
        name="attend",
    )(reach, order, q, kv, after)


def combine_kernel(per_group, *refs):
    parts, table_ref, out_ref = refs[:-2], refs[-2], refs[-1]
    if len(parts) == 1:
        parts = [parts[0].at[e] for e in range(parts[0].shape[0])]
    height, width = parts[0].shape
    rows = height - 32
    tokens = rows // per_group
    lse = []
    for part in parts:
        tail = part[pl.ds(rows, 32), :].astype(jnp.float32)
        lse.append(tail[0:8] + tail[8:16] + tail[16:24])
    top = functools.reduce(jnp.maximum, lse)
    weights = [jnp.exp2(x - top) for x in lse]
    total = functools.reduce(jnp.add, weights)
    weights = jnp.concatenate([w / total for w in weights], axis=0).T
    attended = []
    for h in range(per_group):
        one = jnp.zeros((tokens, width), jnp.float32)
        for e, part in enumerate(parts):
            value = part[pl.ds(h * tokens, tokens), :].astype(jnp.float32)
            one = one + value * weights[:tokens, e * 8 + h : e * 8 + h + 1]
        attended.append(one)
    attended = jnp.concatenate(attended, axis=0)
    high = attended.astype(jnp.bfloat16)
    low = (attended - high.astype(jnp.float32)).astype(jnp.bfloat16)
    restored = jnp.dot(high, table_ref[...], preferred_element_type=jnp.float32)
    restored = restored + jnp.dot(low, table_ref[...], preferred_element_type=jnp.float32)
    restored = (restored * (1.0 / math.sqrt(width))).astype(jnp.bfloat16)
    for h in range(per_group):
        out_ref[:, h * width : (h + 1) * width] = restored[h * tokens : (h + 1) * tokens]


def combine(parts, table, per_group):
    height, width = parts[0].shape[-2:]
    tokens = (height - 32) // per_group
    return pl.pallas_call(
        functools.partial(combine_kernel, per_group),
        out_shape=jax.ShapeDtypeStruct((tokens, per_group * width), jnp.bfloat16),
        compiler_params=pltpu.CompilerParams(vmem_limit_bytes=VMEM_LIMIT),
        name="combine",
    )(*parts, table)


def on_device(queries, cache_codes, cache_scales, pattern, out_weight):
    ny, nx, nz = (lax.axis_size(a) for a in (Y, X, Z))
    y, x, z = (lax.axis_index(a) for a in (Y, X, Z))
    plane = ny * nx
    block_rows = queries.shape[0]
    _, groups, shard_len, width = cache_codes.shape
    heads = queries.shape[1] // width
    per_group = heads // groups
    pages = pattern.shape[2]
    page = shard_len // pages
    blocks = pattern.shape[1]
    total_len = shard_len * blocks
    total_q = block_rows * blocks
    table = hadamard(width)

    marks = pattern.reshape(groups, plane, 1, nz * pages).astype(jnp.bfloat16)
    marks = jnp.transpose(marks, (1, 2, 0, 3)).reshape(plane, 1, -1)
    marks = jnp.pad(marks, ((0, 0), (0, 15), (0, width - marks.shape[2])))

    rotated = rotate(queries, table.astype(jnp.bfloat16), groups)
    q = lax.all_gather(rotated, Z, axis=0, tiled=False)
    weight_rows = lax.all_gather(passed_after(out_weight.T, q), Z, axis=0, tiled=True)

    shards = [dequantize(g, cache_codes, cache_scales, marks, rotated) for g in range(groups)]
    gathered = [lax.all_to_all(shards[0], PLANE, 0, 0)]

    def moved(block, step):
        return lax.ppermute(block, Z, [(i, (i + step) % nz) for i in range(nz)])

    at = (z - jnp.arange(nz, dtype=jnp.int32)) % nz
    first_query = total_len - total_q + ((y * nx + x) * nz + at) * block_rows

    kept = gathered[0][:, 2 * shard_len, : groups * nz * pages].astype(jnp.float32)
    kept = kept.reshape(plane, groups, nz, pages)
    kept = jnp.transpose(kept, (1, 0, 3, 2))
    kept = jnp.flip(jnp.roll(kept, nz - 1 - z, axis=3), axis=3)
    shard = jnp.arange(plane, dtype=jnp.int32) * nz + z
    first_key = shard[:, None] * shard_len + jnp.arange(pages, dtype=jnp.int32) * page
    causal = jnp.clip(first_query[None, None, :] - first_key[:, :, None], -2 * page, 2 * page)
    reach = jnp.where(kept > 0.5, causal[None], -2 * page).reshape(groups, -1)

    gathered.append(lax.all_to_all(tied(shards[1], reach), PLANE, 0, 0))

    parts = attend(q, gathered[0], 0, per_group, reach[0], at, False, q)
    received = [parts[0]] + [moved(parts[i], -i) for i in range(1, nz)]
    packed = attend(q, gathered[1], 1, per_group, reach[1], at, True, parts[0])
    packed = lax.all_to_all(packed, Z, 0, 0)
    signs = table.astype(jnp.bfloat16)
    restored = [combine(received, signs, per_group), combine([packed], signs, per_group)]
    restored = jnp.concatenate(restored, axis=1)
    restored = jnp.broadcast_to(restored[None], (plane,) + restored.shape)
    restored = lax.all_to_all(restored, PLANE, 0, 0)
    terms = lax.dot_general(
        restored.reshape(plane * block_rows, heads * width),
        weight_rows,
        (((1,), (1,)), ((), ())),
        preferred_element_type=jnp.float32,
    ).astype(jnp.bfloat16)
    columns = terms.shape[1]
    terms = lax.all_to_all(terms.reshape(ny, nx, block_rows, columns), GRP, 0, 0)
    share = jnp.sum(terms.astype(jnp.float32), axis=0).astype(jnp.bfloat16)

    same = lax.dynamic_index_in_dim(share, x, 0, keepdims=False)
    other = lax.dynamic_index_in_dim(share, 1 - x, 0, keepdims=False)
    where = [(a, b, c) for a in range(ny) for b in range(nx) for c in range(ny)]

    def flat(a, b, c):
        return (a * nx + b) * ny + c

    same = lax.ppermute(
        same, (Y, X) + GRP, [(flat(a, b, c), flat(c, b, a)) for a, b, c in where]
    )
    other = lax.ppermute(
        other, (Y, X) + GRP, [(flat(a, b, c), flat(c, 1 - b, a)) for a, b, c in where]
    )
    left = jnp.where(x == 0, same, other)
    right = jnp.where(x == 0, other, same)
    return jnp.concatenate([left, right], axis=1)


def solution(mesh):
    parts = Mesh(mesh.devices.reshape(4, 2, 8, 2, 2), (Y, X, Z) + GRP)
    ctx = (Y, X, Z)
    placed = (
        P(ctx, GRP),
        P(None, GRP, ctx, None),
        P(None, GRP, None, ctx),
        P(GRP, None, ctx),
        P(GRP, ctx),
    )
    return jax.shard_map(
        on_device, mesh=parts, in_specs=placed, out_specs=P(ctx, GRP), check_vma=False
    )
```

```python
import functools
import math

import jax
import jax.numpy as jnp
from jax import lax
from jax.experimental import pallas as pl
from jax.experimental.pallas import tpu as pltpu
from jax.sharding import Mesh
from jax.sharding import PartitionSpec as P

NEG_FILL = -1e30
LOG2E = math.log2(math.e)
VMEM_LIMIT = 58 * 1024 * 1024

Y, X, Z = "y", "x_lo", "z"
PLANE = (Y, X)
GRP = ("x_hi", "core")


def hadamard(order):
    index = jnp.arange(order, dtype=jnp.int32)
    common = index[:, None] & index[None, :]
    parity = jnp.zeros((order, order), jnp.int32)
    for shift_bit in range(int(order).bit_length()):
        parity = parity ^ common >> shift_bit & 1
    return jnp.where(parity == 1, -1.0, 1.0).astype(jnp.float32)


def dequantize_kernel(codes_ref, scales_ref, marks_ref, after_ref, out):
    kinds, groups, length, width = codes_ref.shape
    parts = scales_ref.shape[2]
    for g in range(groups):
        for kind in range(kinds):
            scales = scales_ref[kind, g]
            spread = jnp.concatenate(
                [
                    jnp.broadcast_to(scales[i : i + 1], (width // parts, length))
                    for i in range(parts)
                ],
                axis=0,
            )
            values = (codes_ref[kind, g].astype(jnp.float32) - 7.5) * spread.T
            values = values.astype(jnp.bfloat16)
            for copy in range(out.shape[0]):
                out[copy, pl.ds((g * kinds + kind) * length, length), :] = values
    for copy in range(out.shape[0]):
        out[copy, pl.ds(groups * kinds * length, 16), :] = marks_ref[copy]


def dequantize(codes, scales, marks, after):
    kinds, groups, length, width = codes.shape
    shape = (marks.shape[0], groups * kinds * length + 16, width)
    whole = pl.BlockSpec(memory_space=pltpu.VMEM)
    return pl.pallas_call(
        dequantize_kernel,
        in_specs=[whole, whole, whole, pl.BlockSpec(memory_space=pl.ANY)],
        out_shape=jax.ShapeDtypeStruct(shape, jnp.bfloat16),
        compiler_params=pltpu.CompilerParams(vmem_limit_bytes=VMEM_LIMIT),
        name="dequantize",
    )(codes, scales, marks, after)


def rotate_kernel(queries_ref, table_ref, out_ref):
    groups, rows, width = out_ref.shape
    tokens = queries_ref.shape[0]
    per_group = rows // tokens
    scale = LOG2E / width
    for h in range(groups * per_group):
        turned = jnp.dot(
            queries_ref[:, h * width : (h + 1) * width],
            table_ref[...],
            preferred_element_type=jnp.float32,
        )
        at = pl.ds(h % per_group * tokens, tokens)
        out_ref[h // per_group, at, :] = (turned * scale).astype(jnp.bfloat16)


def rotate(queries, table, groups):
    tokens, columns = queries.shape
    width = table.shape[0]
    rows = columns // width // groups * tokens
    return pl.pallas_call(
        rotate_kernel,
        out_shape=jax.ShapeDtypeStruct((groups, rows, width), jnp.bfloat16),
        compiler_params=pltpu.CompilerParams(vmem_limit_bytes=VMEM_LIMIT),
        name="rotate",
    )(queries, table)


def attend_kernel(per_group, unit, page, blocks, reach_ref, order_ref, *refs):
    q_refs, kv_ref, after_ref, packed_ref = refs[: blocks // 2], *refs[blocks // 2 : blocks // 2 + 3]
    pages_ref, s_ref, top_ref, sum_ref, acc_ref = refs[blocks // 2 + 3 :]
    _, _, rows, width = q_refs[0].shape
    tokens = rows // per_group
    sources, height, _ = kv_ref.shape
    length = height // 2
    shard_pages = length // page
    all_pages = sources * shard_pages
    masked_at = all_pages + unit

    def place(p, counts):
        full, some = counts
        reaches = [reach_ref[p * blocks + b] for b in range(blocks)]
        low = functools.reduce(jnp.minimum, reaches)
        high = functools.reduce(jnp.maximum, reaches)
        pages_ref[full] = p
        pages_ref[masked_at + some] = p
        whole = low >= page - 1
        part = jnp.logical_and(high > -tokens, low < page - 1)
        return full + whole.astype(jnp.int32), some + part.astype(jnp.int32)

    start = (jnp.int32(0), jnp.int32(0))
    full, some = lax.fori_loop(0, all_pages, place, start, unroll=4)
    whole = full // unit

    def leftover(i, some):
        pages_ref[masked_at + some] = pages_ref[whole * unit + i]
        return some + 1

    some = lax.fori_loop(0, full - whole * unit, leftover, some)
    rounds = (some + unit - 1) // unit

    def pad(i, _):
        pages_ref[masked_at + some + i] = -1
        return 0

    lax.fori_loop(0, rounds * unit - some, pad, 0)

    ahead = lax.broadcasted_iota(jnp.int32, (tokens, page), 1) - lax.broadcasted_iota(
        jnp.int32, (tokens, page), 0
    )
    top_ref[...] = jnp.full(top_ref.shape, NEG_FILL, jnp.float32)
    sum_ref[...] = jnp.zeros(sum_ref.shape, jnp.float32)
    acc_ref[...] = jnp.zeros(acc_ref.shape, jnp.float32)

    def fetch(p, at):
        first = pl.multiple_of(at + p % shard_pages * page, page)
        return kv_ref[p // shard_pages, pl.ds(first, page), :]

    def first_pass(i, base, slot, masked):
        ps = [pages_ref[base + i * unit + u] for u in range(unit)]
        held = [jnp.maximum(p, 0) for p in ps]
        k = jnp.concatenate([fetch(p, 0) for p in held], axis=0)
        for b in range(blocks):
            at = pl.ds(b * rows, rows)
            s = lax.dot_general(
                q_refs[b // 2][b % 2, 0], k, (((1,), (1,)), ((), ())), preferred_element_type=jnp.float32
            )
            top = top_ref[at, :]
            for u in range(unit):
                x = s[:, u * page : (u + 1) * page]
                if masked:
                    reach = jnp.where(ps[u] < 0, -2 * page, reach_ref[held[u] * blocks + b])
                    x = x.reshape(per_group, tokens, page)
                    x = jnp.where((ahead <= reach)[None], x, NEG_FILL).reshape(rows, page)
                s_ref[slot, at, u * page : (u + 1) * page] = x
                top = jnp.maximum(top, x)
            top_ref[at, :] = top
        return 0

    def second_pass(i, base, slot):
        held = [jnp.maximum(pages_ref[base + i * unit + u], 0) for u in range(unit)]
        v = jnp.concatenate([fetch(p, length) for p in held], axis=0)
        for b in range(blocks):
            at = pl.ds(b * rows, rows)
            top = top_ref[at, :]
            weights = [
                jnp.exp2(s_ref[slot, at, u * page : (u + 1) * page] - top) for u in range(unit)
            ]
            sum_ref[at, :] = sum_ref[at, :] + functools.reduce(jnp.add, weights)
            weights = jnp.concatenate([w.astype(jnp.bfloat16) for w in weights], axis=1)
            acc_ref[at, :] = acc_ref[at, :] + jnp.dot(
                weights, v, preferred_element_type=jnp.float32
            )
        return 0

    lax.fori_loop(0, whole, lambda i, _: first_pass(i, 0, i, False), 0)
    lax.fori_loop(0, rounds, lambda i, _: first_pass(i, masked_at, whole + i, True), 0)
    for b in range(blocks):
        at = pl.ds(b * rows, rows)
        top = jnp.max(top_ref[at, :], axis=1, keepdims=True)
        top_ref[at, :] = jnp.broadcast_to(top, (rows, page))
    lax.fori_loop(0, whole, lambda i, _: second_pass(i, 0, i), 0)
    lax.fori_loop(0, rounds, lambda i, _: second_pass(i, masked_at, whole + i), 0)
    for b in range(blocks):
        at = pl.ds(b * rows, rows)
        total = jnp.sum(sum_ref[at, :], axis=1, keepdims=True)
        total = jnp.maximum(total, 1e-30)
        out = (acc_ref[at, :] / total).astype(jnp.bfloat16)
        lse = top_ref[at, :] + jnp.log2(total)
        across = [
            jnp.sum(
                jnp.where(ahead == 0, lse[h * tokens : (h + 1) * tokens], 0.0),
                axis=0,
                keepdims=True,
            )
            for h in range(per_group)
        ]
        across.append(jnp.zeros((8 - per_group, page), jnp.float32))
        across = jnp.concatenate(across, axis=0)
        high = across.astype(jnp.bfloat16).astype(jnp.float32)
        middle = (across - high).astype(jnp.bfloat16).astype(jnp.float32)
        low = across - high - middle
        tail = jnp.concatenate([high, middle, low, jnp.zeros_like(low)], axis=0)
        tail = tail.astype(jnp.bfloat16)
        packed_ref[order_ref[b], pl.ds(0, rows), :] = out
        packed_ref[order_ref[b], pl.ds(rows, 32), :] = tail


def attend(q_pairs, kv, g, per_group, reach, order, after):
    blocks = 2 * len(q_pairs)
    _, groups, rows, width = q_pairs[0].shape
    sources, height, _ = kv.shape
    height = (height - 16) // groups
    page = 128
    pages = sources * (height // 2 // page)
    unit = 4
    packed = (blocks, rows + 32, width)
    scores = blocks * rows * pages * page // 2
    once = pl.Buffered(1)
    return pl.pallas_call(
        functools.partial(attend_kernel, per_group, unit, page, blocks),
        grid_spec=pltpu.PrefetchScalarGridSpec(
            num_scalar_prefetch=2,
            grid=(1,),
            in_specs=[
                pl.BlockSpec(
                    (2, 1, rows, width), lambda t, *_: (0, g, 0, 0), pipeline_mode=once
                )
            ]
            * len(q_pairs)
            + [
                pl.BlockSpec(
                    (sources, height, width), lambda t, *_: (0, g, 0), pipeline_mode=once
                ),
                pl.BlockSpec(memory_space=pl.ANY),
            ],
            out_specs=pl.BlockSpec(packed, lambda t, *_: (0, 0, 0)),
            scratch_shapes=[
                pltpu.SMEM((2 * (pages + unit),), jnp.int32),
                pltpu.VMEM((pages // unit + 1, blocks * rows, unit * page), jnp.float32),
                pltpu.VMEM((blocks * rows, page), jnp.float32),
                pltpu.VMEM((blocks * rows, page), jnp.float32),
                pltpu.VMEM((blocks * rows, width), jnp.float32),
            ],
        ),
        out_shape=jax.ShapeDtypeStruct(packed, jnp.bfloat16),
        compiler_params=pltpu.CompilerParams(vmem_limit_bytes=VMEM_LIMIT),
        cost_estimate=pl.CostEstimate(
            flops=8 * scores * width, bytes_accessed=8 * 1024 * 1024, transcendentals=scores
        ),
        name="attend",
    )(reach, order, *q_pairs, kv, after)


def combine_kernel(per_group, parts_ref, table_ref, after_ref, out_ref):
    sources, height, width = parts_ref.shape
    parts = [parts_ref.at[e] for e in range(sources)]
    rows = height - 32
    tokens = rows // per_group
    lse = []
    for part in parts:
        tail = part[pl.ds(rows, 32), :].astype(jnp.float32)
        lse.append(tail[0:8] + tail[8:16] + tail[16:24])
    top = functools.reduce(jnp.maximum, lse)
    weights = [jnp.exp2(x - top) for x in lse]
    total = functools.reduce(jnp.add, weights)
    weights = jnp.concatenate([w / total for w in weights], axis=0).T
    attended = []
    for h in range(per_group):
        one = jnp.zeros((tokens, width), jnp.float32)
        for e, part in enumerate(parts):
            value = part[pl.ds(h * tokens, tokens), :].astype(jnp.float32)
            one = one + value * weights[:tokens, e * 8 + h : e * 8 + h + 1]
        attended.append(one)
    attended = jnp.concatenate(attended, axis=0)
    high = attended.astype(jnp.bfloat16)
    low = (attended - high.astype(jnp.float32)).astype(jnp.bfloat16)
    restored = jnp.dot(high, table_ref[...], preferred_element_type=jnp.float32)
    restored = restored + jnp.dot(low, table_ref[...], preferred_element_type=jnp.float32)
    restored = (restored * (1.0 / math.sqrt(width))).astype(jnp.bfloat16)
    for copy in range(out_ref.shape[0]):
        for h in range(per_group):
            part = restored[h * tokens : (h + 1) * tokens]
            out_ref[copy, :, h * width : (h + 1) * width] = part


def combine(parts, table, per_group, copies, after):
    _, height, width = parts.shape
    tokens = (height - 32) // per_group
    whole = pl.BlockSpec(memory_space=pltpu.VMEM)
    return pl.pallas_call(
        functools.partial(combine_kernel, per_group),
        in_specs=[whole, whole, pl.BlockSpec(memory_space=pl.ANY)],
        out_shape=jax.ShapeDtypeStruct((copies, tokens, per_group * width), jnp.bfloat16),
        compiler_params=pltpu.CompilerParams(vmem_limit_bytes=VMEM_LIMIT),
        name="combine",
    )(parts, table, after)


def project_kernel(plane, place_ref, *refs):
    firsts, second_ref, weights_ref, out_ref, rows_ref = refs[: plane // 2], *refs[plane // 2 :]
    tokens, half = firsts[0].shape[-2:]
    for d in range(plane):
        source = place_ref[0] ^ d
        at = pl.ds(pl.multiple_of(source * tokens, tokens), tokens)
        rows_ref[at, pl.ds(0, half)] = firsts[d // 2][d % 2]
    for e in range(plane):
        rows_ref[pl.ds(e * tokens, tokens), pl.ds(half, half)] = second_ref[e]
    terms = lax.dot_general(
        rows_ref[...], weights_ref[...], (((1,), (1,)), ((), ())), preferred_element_type=jnp.float32
    )
    out_ref[...] = terms.astype(jnp.bfloat16).reshape(out_ref.shape)


def project(firsts, second, weights, place):
    plane, tokens, half = second.shape
    columns = weights.shape[0]
    whole = pl.BlockSpec(memory_space=pltpu.VMEM)
    return pl.pallas_call(
        functools.partial(project_kernel, plane),
        in_specs=[pl.BlockSpec(memory_space=pltpu.SMEM)] + [whole] * (len(firsts) + 2),
        out_shape=jax.ShapeDtypeStruct((plane, tokens, columns), jnp.bfloat16),
        scratch_shapes=[pltpu.VMEM((plane * tokens, 2 * half), jnp.bfloat16)],
        compiler_params=pltpu.CompilerParams(vmem_limit_bytes=VMEM_LIMIT),
        name="project",
    )(place, *firsts, second, weights)


def on_device(queries, cache_codes, cache_scales, pattern, out_weight):
    ny, nx, nz = (lax.axis_size(a) for a in (Y, X, Z))
    y, x, z = (lax.axis_index(a) for a in (Y, X, Z))
    plane = ny * nx
    block_rows = queries.shape[0]
    _, groups, shard_len, width = cache_codes.shape
    heads = queries.shape[1] // width
    per_group = heads // groups
    pages = pattern.shape[2]
    page = shard_len // pages
    blocks = pattern.shape[1]
    total_len = shard_len * blocks
    total_q = block_rows * blocks
    table = hadamard(width)

    marks = pattern.reshape(groups, plane, 1, nz * pages).astype(jnp.bfloat16)
    marks = jnp.transpose(marks, (1, 2, 0, 3)).reshape(plane, 1, -1)
    marks = jnp.pad(marks, ((0, 0), (0, 15), (0, width - marks.shape[2])))

    weight_rows = lax.all_gather(out_weight.T, Z, axis=0, tiled=True)
    rotated = rotate(queries, table.astype(jnp.bfloat16), groups)
    shards = dequantize(cache_codes, cache_scales, marks, rotated)
    kv = lax.all_to_all(shards, PLANE, 0, 0)

    def moved(block, step):
        return lax.ppermute(block, Z, [(i, (i + step) % nz) for i in range(nz)])

    pair = jnp.stack([rotated, moved(rotated, nz // 2)])
    steps = [0, 1, -1, 2]
    q_pairs = [pair] + [moved(pair, step) for step in steps[1:]]
    back = jnp.array([s + far for s in steps for far in (0, nz // 2)], jnp.int32)
    at = (z - back) % nz
    first_query = total_len - total_q + ((y * nx + x) * nz + at) * block_rows

    kept = kv[:, 2 * groups * shard_len, : groups * nz * pages].astype(jnp.float32)
    kept = kept.reshape(plane, groups, nz, pages)
    kept = jnp.transpose(kept, (1, 0, 3, 2))
    kept = sum(
        jnp.where(at == i, kept[..., i : i + 1], 0.0) for i in range(nz)
    )
    shard = jnp.arange(plane, dtype=jnp.int32) * nz + z
    first_key = shard[:, None] * shard_len + jnp.arange(pages, dtype=jnp.int32) * page
    causal = jnp.clip(first_query[None, None, :] - first_key[:, :, None], -2 * page, 2 * page)
    reach = jnp.where(kept > 0.5, causal[None], -2 * page).reshape(groups, -1)

    signs = table.astype(jnp.bfloat16)
    packed = attend(q_pairs, kv, 0, per_group, reach[0], at, kv)
    first = lax.all_to_all(packed, Z, 0, 0)
    packed = attend(q_pairs, kv, 1, per_group, reach[1], at, weight_rows)
    second = lax.all_to_all(packed, Z, 0, 0)
    first = combine(first, signs, per_group, 1, first)
    beside = lax.ppermute(first, PLANE, [(e, e ^ 1) for e in range(plane)])
    first = jnp.concatenate([first, beside], axis=0)
    firsts = [first]
    for d in range(2, plane, 2):
        firsts.append(lax.ppermute(first, PLANE, [(e, e ^ d) for e in range(plane)]))
    second = combine(second, signs, per_group, plane, sum(f[0, 0, :1] for f in firsts))
    second = lax.all_to_all(second, PLANE, 0, 0)
    place = (y * nx + x).astype(jnp.int32).reshape(1)
    terms = project(firsts, second, weight_rows, place)
    columns = terms.shape[2]
    terms = lax.all_to_all(terms.reshape(ny, nx, block_rows, columns), GRP, 0, 0)
    share = jnp.sum(terms.astype(jnp.float32), axis=0).astype(jnp.bfloat16)

    same = lax.dynamic_index_in_dim(share, x, 0, keepdims=False)
    other = lax.dynamic_index_in_dim(share, 1 - x, 0, keepdims=False)
    where = [(a, b, c) for a in range(ny) for b in range(nx) for c in range(ny)]

    def flat(a, b, c):
        return (a * nx + b) * ny + c

    same = lax.ppermute(
        same, (Y, X) + GRP, [(flat(a, b, c), flat(c, b, a)) for a, b, c in where]
    )
    other = lax.ppermute(
        other, (Y, X) + GRP, [(flat(a, b, c), flat(c, 1 - b, a)) for a, b, c in where]
    )
    left = jnp.where(x == 0, same, other)
    right = jnp.where(x == 0, other, same)
    return jnp.concatenate([left, right], axis=1)


def solution(mesh):
    parts = Mesh(mesh.devices.reshape(4, 2, 8, 2, 2), (Y, X, Z) + GRP)
    ctx = (Y, X, Z)
    placed = (
        P(ctx, GRP),
        P(None, GRP, ctx, None),
        P(None, GRP, None, ctx),
        P(GRP, None, ctx),
        P(GRP, ctx),
    )
    return jax.shard_map(
        on_device, mesh=parts, in_specs=placed, out_specs=P(ctx, GRP), check_vma=False
    )
```

```python
import functools
import math

import jax
import jax.numpy as jnp
from jax import lax
from jax.experimental import pallas as pl
from jax.experimental.pallas import tpu as pltpu
from jax.sharding import Mesh
from jax.sharding import PartitionSpec as P

NEG_FILL = -1e30
LOG2E = math.log2(math.e)
VMEM_LIMIT = 60 * 1024 * 1024

Y, X, Z = "y", "x_lo", "z"
PLANE = (Y, X)
GRP = ("x_hi", "core")


def hadamard(order):
    index = jnp.arange(order, dtype=jnp.int32)
    common = index[:, None] & index[None, :]
    parity = jnp.zeros((order, order), jnp.int32)
    for shift_bit in range(int(order).bit_length()):
        parity = parity ^ common >> shift_bit & 1
    return jnp.where(parity == 1, -1.0, 1.0).astype(jnp.float32)


def dequantize_kernel(codes_ref, scales_ref, out):
    kinds, groups, length, width = codes_ref.shape
    parts = scales_ref.shape[2]
    for g in range(groups):
        for kind in range(kinds):
            scales = scales_ref[kind, g]
            spread = jnp.concatenate(
                [
                    jnp.broadcast_to(scales[i : i + 1], (width // parts, length))
                    for i in range(parts)
                ],
                axis=0,
            )
            values = (codes_ref[kind, g].astype(jnp.float32) - 7.5) * spread.T
            values = values.astype(jnp.bfloat16)
            for copy in range(out.shape[0]):
                out[copy, pl.ds((g * kinds + kind) * length, length), :] = values


def dequantize(codes, scales, copies):
    kinds, groups, length, width = codes.shape
    shape = (copies, groups * kinds * length, width)
    return pl.pallas_call(
        dequantize_kernel,
        out_shape=jax.ShapeDtypeStruct(shape, jnp.bfloat16),
        compiler_params=pltpu.CompilerParams(vmem_limit_bytes=VMEM_LIMIT),
        name="dequantize",
    )(codes, scales)


def tie_kernel(block_ref, after_ref, out_ref):
    pass


def tied(block, after):
    anywhere = pl.BlockSpec(memory_space=pl.ANY)
    return pl.pallas_call(
        tie_kernel,
        in_specs=[anywhere, anywhere],
        out_specs=anywhere,
        out_shape=jax.ShapeDtypeStruct(block.shape, block.dtype),
        input_output_aliases={0: 0},
        name="tie",
    )(block, after)


def rotate_kernel(queries_ref, table_ref, out_ref):
    groups, rows, width = out_ref.shape
    tokens = queries_ref.shape[0]
    per_group = rows // tokens
    scale = LOG2E / width
    for h in range(groups * per_group):
        turned = jnp.dot(
            queries_ref[:, h * width : (h + 1) * width],
            table_ref[...],
            preferred_element_type=jnp.float32,
        )
        at = pl.ds(h % per_group * tokens, tokens)
        out_ref[h // per_group, at, :] = (turned * scale).astype(jnp.bfloat16)


def rotate(queries, table, groups):
    tokens, columns = queries.shape
    width = table.shape[0]
    rows = columns // width // groups * tokens
    return pl.pallas_call(
        rotate_kernel,
        out_shape=jax.ShapeDtypeStruct((groups, rows, width), jnp.bfloat16),
        compiler_params=pltpu.CompilerParams(vmem_limit_bytes=VMEM_LIMIT),
        name="rotate",
    )(queries, table)


def attend_kernel(per_group, unit, page, held, reach_ref, order_ref, *refs):
    q_refs, kv_ref, packed_ref = refs[: len(held)], *refs[len(held) : len(held) + 2]
    pages_ref, s_ref, top_ref, sum_ref, acc_ref = refs[len(held) + 2 :]
    queries = [ref.at[i, 0] for ref, n in zip(q_refs, held) for i in range(n)]
    blocks = len(queries)
    rows, width = queries[0].shape
    tokens = rows // per_group
    sources, height, _ = kv_ref.shape
    length = height // 2
    shard_pages = length // page
    all_pages = sources * shard_pages
    masked_at = all_pages + unit
    group_at = pl.program_id(0) * all_pages

    def place(p, counts):
        full, some = counts
        reaches = [reach_ref[(group_at + p) * blocks + b] for b in range(blocks)]
        low = functools.reduce(jnp.minimum, reaches)
        high = functools.reduce(jnp.maximum, reaches)
        pages_ref[full] = p
        pages_ref[masked_at + some] = p
        whole = low >= page - 1
        part = jnp.logical_and(high > -tokens, low < page - 1)
        return full + whole.astype(jnp.int32), some + part.astype(jnp.int32)

    start = (jnp.int32(0), jnp.int32(0))
    full, some = lax.fori_loop(0, all_pages, place, start, unroll=4)
    whole = full // unit

    def leftover(i, some):
        pages_ref[masked_at + some] = pages_ref[whole * unit + i]
        return some + 1

    some = lax.fori_loop(0, full - whole * unit, leftover, some)
    rounds = (some + unit - 1) // unit

    def pad(i, _):
        pages_ref[masked_at + some + i] = -1
        return 0

    lax.fori_loop(0, rounds * unit - some, pad, 0)

    ahead = lax.broadcasted_iota(jnp.int32, (tokens, page), 1) - lax.broadcasted_iota(
        jnp.int32, (tokens, page), 0
    )
    top_ref[...] = jnp.full(top_ref.shape, NEG_FILL, jnp.float32)
    sum_ref[...] = jnp.zeros(sum_ref.shape, jnp.float32)
    acc_ref[...] = jnp.zeros(acc_ref.shape, jnp.float32)

    def fetch(p, at):
        first = pl.multiple_of(at + p % shard_pages * page, page)
        return kv_ref[p // shard_pages, pl.ds(first, page), :]

    def first_pass(i, base, slot, masked):
        ps = [pages_ref[base + i * unit + u] for u in range(unit)]
        pages_at = [jnp.maximum(p, 0) for p in ps]
        k = jnp.concatenate([fetch(p, 0) for p in pages_at], axis=0)
        for b in range(blocks):
            at = pl.ds(b * rows, rows)
            s = lax.dot_general(
                queries[b][...], k, (((1,), (1,)), ((), ())), preferred_element_type=jnp.float32
            )
            top = top_ref[at, :]
            for u in range(unit):
                x = s[:, u * page : (u + 1) * page]
                if masked:
                    reach = jnp.where(ps[u] < 0, -2 * page, reach_ref[(group_at + pages_at[u]) * blocks + b])
                    x = x.reshape(per_group, tokens, page)
                    x = jnp.where((ahead <= reach)[None], x, NEG_FILL).reshape(rows, page)
                s_ref[slot, at, u * page : (u + 1) * page] = x
                top = jnp.maximum(top, x)
            top_ref[at, :] = top
        return 0

    def second_pass(i, base, slot):
        pages_at = [jnp.maximum(pages_ref[base + i * unit + u], 0) for u in range(unit)]
        v = jnp.concatenate([fetch(p, length) for p in pages_at], axis=0)
        for b in range(blocks):
            at = pl.ds(b * rows, rows)
            top = top_ref[at, :]
            weights = [
                jnp.exp2(s_ref[slot, at, u * page : (u + 1) * page] - top) for u in range(unit)
            ]
            sum_ref[at, :] = sum_ref[at, :] + functools.reduce(jnp.add, weights)
            weights = jnp.concatenate([w.astype(jnp.bfloat16) for w in weights], axis=1)
            acc_ref[at, :] = acc_ref[at, :] + jnp.dot(
                weights, v, preferred_element_type=jnp.float32
            )
        return 0

    lax.fori_loop(0, whole, lambda i, _: first_pass(i, 0, i, False), 0)
    lax.fori_loop(0, rounds, lambda i, _: first_pass(i, masked_at, whole + i, True), 0)
    for b in range(blocks):
        at = pl.ds(b * rows, rows)
        top = jnp.max(top_ref[at, :], axis=1, keepdims=True)
        top_ref[at, :] = jnp.broadcast_to(top, (rows, page))
    lax.fori_loop(0, whole, lambda i, _: second_pass(i, 0, i), 0)
    lax.fori_loop(0, rounds, lambda i, _: second_pass(i, masked_at, whole + i), 0)
    for b in range(blocks):
        at = pl.ds(b * rows, rows)
        total = jnp.sum(sum_ref[at, :], axis=1, keepdims=True)
        total = jnp.maximum(total, 1e-30)
        out = (acc_ref[at, :] / total).astype(jnp.bfloat16)
        lse = top_ref[at, :] + jnp.log2(total)
        across = [
            jnp.sum(
                jnp.where(ahead == 0, lse[h * tokens : (h + 1) * tokens], 0.0),
                axis=0,
                keepdims=True,
            )
            for h in range(per_group)
        ]
        across.append(jnp.zeros((8 - per_group, page), jnp.float32))
        across = jnp.concatenate(across, axis=0)
        high = across.astype(jnp.bfloat16).astype(jnp.float32)
        middle = (across - high).astype(jnp.bfloat16).astype(jnp.float32)
        low = across - high - middle
        tail = jnp.concatenate([high, middle, low, jnp.zeros_like(low)], axis=0)
        tail = tail.astype(jnp.bfloat16)
        packed_ref[order_ref[b], 0, pl.ds(0, rows), :] = out
        packed_ref[order_ref[b], 0, pl.ds(rows, 32), :] = tail


def attend(queries, kv, per_group, reach, order):
    held = [q.shape[0] for q in queries]
    blocks = sum(held)
    _, groups, rows, width = queries[0].shape
    sources, height, _ = kv.shape
    height = height // groups
    page = 128
    pages = sources * (height // 2 // page)
    unit = 4
    packed = (blocks, groups, rows + 32, width)
    scores = blocks * groups * rows * pages * page // 2
    return pl.pallas_call(
        functools.partial(attend_kernel, per_group, unit, page, held),
        grid_spec=pltpu.PrefetchScalarGridSpec(
            num_scalar_prefetch=2,
            grid=(groups,),
            in_specs=[pl.BlockSpec((n, 1, rows, width), lambda g, *_: (0, g, 0, 0)) for n in held]
            + [pl.BlockSpec((sources, height, width), lambda g, *_: (0, g, 0))],
            out_specs=pl.BlockSpec((blocks, 1, rows + 32, width), lambda g, *_: (0, g, 0, 0)),
            scratch_shapes=[
                pltpu.SMEM((2 * (pages + unit),), jnp.int32),
                pltpu.VMEM((pages // unit + 1, blocks * rows, unit * page), jnp.float32),
                pltpu.VMEM((blocks * rows, page), jnp.float32),
                pltpu.VMEM((blocks * rows, page), jnp.float32),
                pltpu.VMEM((blocks * rows, width), jnp.float32),
            ],
        ),
        out_shape=jax.ShapeDtypeStruct(packed, jnp.bfloat16),
        compiler_params=pltpu.CompilerParams(vmem_limit_bytes=VMEM_LIMIT),
        cost_estimate=pl.CostEstimate(
            flops=8 * scores * width, bytes_accessed=8 * 1024 * 1024, transcendentals=scores
        ),
        name="attend",
    )(reach, order, *queries, kv)


def combine_kernel(per_group, parts_ref, table_ref, out_ref):
    sources, groups, height, width = parts_ref.shape
    rows = height - 32
    tokens = rows // per_group
    for g in range(groups):
        tails = parts_ref[:, g, pl.ds(rows, 32), :].astype(jnp.float32)
        lse = tails[:, 0:8] + tails[:, 8:16] + tails[:, 16:24]
        weights = jnp.exp2(lse - jnp.max(lse, axis=0, keepdims=True))
        weights = weights / jnp.sum(weights, axis=0, keepdims=True)
        weights = weights.reshape(sources * 8, width).T
        attended = []
        for h in range(per_group):
            one = jnp.zeros((tokens, width), jnp.float32)
            for e in range(sources):
                value = parts_ref[e, g, pl.ds(h * tokens, tokens), :].astype(jnp.float32)
                one = one + value * weights[:tokens, e * 8 + h : e * 8 + h + 1]
            attended.append(one)
        attended = jnp.concatenate(attended, axis=0)
        high = attended.astype(jnp.bfloat16)
        low = (attended - high.astype(jnp.float32)).astype(jnp.bfloat16)
        restored = jnp.dot(high, table_ref[...], preferred_element_type=jnp.float32)
        restored = restored + jnp.dot(low, table_ref[...], preferred_element_type=jnp.float32)
        restored = (restored * (1.0 / math.sqrt(width))).astype(jnp.bfloat16)
        for copy in range(out_ref.shape[0]):
            for h in range(per_group):
                at = (g * per_group + h) * width
                out_ref[copy, :, at : at + width] = restored[h * tokens : (h + 1) * tokens]


def combine(parts, table, per_group, copies):
    _, groups, height, width = parts.shape
    tokens = (height - 32) // per_group
    return pl.pallas_call(
        functools.partial(combine_kernel, per_group),
        out_shape=jax.ShapeDtypeStruct((copies, tokens, groups * per_group * width), jnp.bfloat16),
        compiler_params=pltpu.CompilerParams(vmem_limit_bytes=VMEM_LIMIT),
        name="combine",
    )(parts, table)


def project_kernel(place_ref, rows_ref, own_ref, other_ref, keep_ref, send_ref):
    _, tokens, _ = rows_ref.shape
    columns = own_ref.shape[0]
    x, x_hi, core = place_ref[0], place_ref[1], place_ref[2]
    wanted = [2 * hi + c for c in (core, 1 - core) for hi in (x_hi, 1 - x_hi)]
    rows = jnp.concatenate([rows_ref[i] for i in wanted], axis=0)
    for side, weights_ref in ((x, own_ref), (1 - x, other_ref)):
        at = pl.ds(pl.multiple_of(side * columns, columns), columns)
        terms = lax.dot_general(
            rows, weights_ref[...], (((1,), (1,)), ((), ())), preferred_element_type=jnp.float32
        ).astype(jnp.bfloat16)
        for i in range(2):
            keep_ref[i, :, at] = terms[i * tokens : (i + 1) * tokens]
            send_ref[i, :, at] = terms[(2 + i) * tokens : (3 + i) * tokens]


def project(rows, own, other, place):
    _, tokens, _ = rows.shape
    columns = own.shape[0]
    whole = pl.BlockSpec(memory_space=pltpu.VMEM)
    return pl.pallas_call(
        project_kernel,
        in_specs=[pl.BlockSpec(memory_space=pltpu.SMEM), whole, whole, whole],
        out_shape=[jax.ShapeDtypeStruct((2, tokens, 2 * columns), jnp.bfloat16)] * 2,
        compiler_params=pltpu.CompilerParams(vmem_limit_bytes=VMEM_LIMIT),
        name="project",
    )(place, rows, own, other)


def on_device(queries, cache_codes, cache_scales, pattern, out_weight):
    ny, nx, nz = (lax.axis_size(a) for a in (Y, X, Z))
    y, x, z = (lax.axis_index(a) for a in (Y, X, Z))
    x_hi, core = (lax.axis_index(a) for a in GRP)
    plane = ny * nx
    place = y * nx + x
    block_rows = queries.shape[0]
    _, groups, shard_len, width = cache_codes.shape
    heads = queries.shape[1] // width
    per_group = heads // groups
    pages = pattern.shape[2]
    page = shard_len // pages
    blocks = pattern.shape[1]
    total_len = shard_len * blocks
    total_q = block_rows * blocks
    table = hadamard(width)

    def along(block, step):
        return lax.ppermute(block, Z, [(i, (i + step) % nz) for i in range(nz)])

    def across(block, step):
        return lax.ppermute(block, PLANE, [(e, e ^ step) for e in range(plane)])

    kv = lax.all_to_all(dequantize(cache_codes, cache_scales, plane), PLANE, 0, 0)

    rotated = rotate(queries, table.astype(jnp.bfloat16), groups)
    pair = jnp.stack([rotated, along(rotated, nz // 2)])
    held = [pair, along(pair, 1), along(pair, -1)]
    held += [along(rotated, 2)[None], along(rotated, -2)[None]]
    back = [s + far for s in (0, 1, -1) for far in (0, nz // 2)] + [2, -2]
    at = (z - jnp.array(back, jnp.int32)) % nz
    first_query = total_len - total_q + (place * nz + at) * block_rows

    kept = jnp.stack([pattern, across(pattern, 1)])
    kept = jnp.concatenate([kept] + [across(kept, d) for d in range(2, plane, 2)])
    kept = lax.dynamic_slice_in_dim(kept, place * nz, nz, axis=2)
    shard = jnp.arange(plane, dtype=jnp.int32)
    kept = sum(
        jnp.where((shard ^ place == d)[:, None, None, None], kept[d][None], 0)
        for d in range(plane)
    )
    kept = jnp.transpose(kept, (1, 0, 3, 2))
    kept = sum(jnp.where(at == i, kept[..., i : i + 1], 0) for i in range(nz))
    first_key = (shard * nz + z)[:, None] * shard_len + jnp.arange(pages, dtype=jnp.int32) * page
    causal = jnp.clip(first_query[None, None, :] - first_key[:, :, None], -2 * page, 2 * page)
    reach = jnp.where(kept == 1, causal[None], -2 * page).reshape(-1)

    own = lax.all_gather(out_weight.T, Z, axis=0, tiled=True)
    other = across(own, 1)

    packed = attend(held, kv, per_group, reach, at)
    parts = lax.all_to_all(tied(packed, own[:16, :width]), Z, 0, 0)
    restored = combine(parts, table.astype(jnp.bfloat16), per_group, ny)
    restored = lax.all_to_all(restored, Y, 0, 0)
    here = jnp.stack([x, x_hi, core]).astype(jnp.int32)
    keep, send = project(restored, own, other, here)

    send = lax.ppermute(send, GRP[1], [(0, 1), (1, 0)])
    share = (keep.astype(jnp.float32) + send.astype(jnp.float32)).astype(jnp.bfloat16)
    cores = ny // 2
    where = [(a, b, c) for a in range(ny) for b in range(cores) for c in range(2)]
    mixed = jnp.zeros(share.shape[1:], jnp.float32)
    for i in range(2):
        route = [
            ((a * cores + b) * 2 + c, ((2 * (b ^ i) + c) * cores + a // 2) * 2 + a % 2)
            for a, b, c in where
        ]
        mixed = mixed + lax.ppermute(share[i], (Y,) + GRP, route).astype(jnp.float32)
    return mixed.astype(jnp.bfloat16)


def solution(mesh):
    parts = Mesh(mesh.devices.reshape(4, 2, 8, 2, 2), (Y, X, Z) + GRP)
    ctx = (Y, X, Z)
    placed = (
        P(ctx, GRP),
        P(None, GRP, ctx, None),
        P(None, GRP, None, ctx),
        P(GRP, None, ctx),
        P(GRP, ctx),
    )
    return jax.shard_map(
        on_device, mesh=parts, in_specs=placed, out_specs=P(ctx, GRP), check_vma=False
    )
```

```python
import functools
import math

import jax
import jax.numpy as jnp
from jax import lax
from jax.experimental import pallas as pl
from jax.experimental.pallas import tpu as pltpu
from jax.sharding import Mesh
from jax.sharding import PartitionSpec as P

NEG_FILL = -1e30
LOG2E = math.log2(math.e)
VMEM_LIMIT = 60 * 1024 * 1024

Y, X, Z = "y", "x_lo", "z"
PLANE = (Y, X)
GRP = ("x_hi", "core")


def hadamard(order):
    index = jnp.arange(order, dtype=jnp.int32)
    common = index[:, None] & index[None, :]
    parity = jnp.zeros((order, order), jnp.int32)
    for shift_bit in range(int(order).bit_length()):
        parity = parity ^ common >> shift_bit & 1
    return jnp.where(parity == 1, -1.0, 1.0).astype(jnp.float32)


def dequantize_kernel(codes_ref, scales_ref, marks_ref, out):
    kinds, groups, length, width = codes_ref.shape
    parts = scales_ref.shape[2]
    for g in range(groups):
        for kind in range(kinds):
            scales = scales_ref[kind, g]
            spread = jnp.concatenate(
                [
                    jnp.broadcast_to(scales[i : i + 1], (width // parts, length))
                    for i in range(parts)
                ],
                axis=0,
            )
            values = (codes_ref[kind, g].astype(jnp.float32) - 7.5) * spread.T
            values = values.astype(jnp.bfloat16)
            for copy in range(out.shape[0]):
                out[copy, pl.ds((g * kinds + kind) * length, length), :] = values
    marks = marks_ref[...].astype(jnp.float32)
    marks = jnp.concatenate([marks, jnp.zeros((16 - marks.shape[0], width), jnp.float32)], axis=0)
    for copy in range(out.shape[0]):
        out[copy, pl.ds(kinds * groups * length, 16), :] = marks.astype(jnp.bfloat16)


def dequantize(codes, scales, marks, copies):
    kinds, groups, length, width = codes.shape
    shape = (copies, groups * kinds * length + 16, width)
    return pl.pallas_call(
        dequantize_kernel,
        out_shape=jax.ShapeDtypeStruct(shape, jnp.bfloat16),
        compiler_params=pltpu.CompilerParams(vmem_limit_bytes=VMEM_LIMIT),
        name="dequantize",
    )(codes, scales, marks)


def pass_kernel(block_ref, *refs):
    refs[-1][...] = block_ref[...]


def passed_after(block, *after):
    anywhere = pl.BlockSpec(memory_space=pl.ANY)
    return pl.pallas_call(
        pass_kernel,
        in_specs=[pl.BlockSpec(memory_space=pltpu.VMEM)] + [anywhere] * len(after),
        out_shape=jax.ShapeDtypeStruct(block.shape, block.dtype),
        name="pass",
    )(block, *after)


def rotate_kernel(queries_ref, table_ref, out_ref):
    groups, rows, width = out_ref.shape
    tokens = queries_ref.shape[0]
    per_group = rows // tokens
    scale = LOG2E / width
    for h in range(groups * per_group):
        turned = jnp.dot(
            queries_ref[:, h * width : (h + 1) * width],
            table_ref[...],
            preferred_element_type=jnp.float32,
        )
        at = pl.ds(h % per_group * tokens, tokens)
        out_ref[h // per_group, at, :] = (turned * scale).astype(jnp.bfloat16)


def rotate(queries, table, groups):
    tokens, columns = queries.shape
    width = table.shape[0]
    rows = columns // width // groups * tokens
    return pl.pallas_call(
        rotate_kernel,
        out_shape=jax.ShapeDtypeStruct((groups, rows, width), jnp.bfloat16),
        compiler_params=pltpu.CompilerParams(vmem_limit_bytes=VMEM_LIMIT),
        name="rotate",
    )(queries, table)


def attend_kernel(per_group, unit, page, held, starts, order_ref, *refs):
    q_refs, kv_ref, marks_ref, packed_ref = refs[: len(held)], *refs[len(held) : len(held) + 3]
    reach_ref, pages_ref, mask_ref, s_ref, top_ref, sum_ref, acc_ref = refs[len(held) + 3 :]
    queries = [ref.at[i, 0] for ref, n in zip(q_refs, held) for i in range(n)]
    blocks = len(queries)
    rows, width = queries[0].shape
    tokens = rows // per_group
    sources, height, _ = kv_ref.shape
    length = height // 2
    shard_pages = length // page
    all_pages = sources * shard_pages
    masked_at = all_pages + unit
    g = pl.program_id(0)
    place, z = order_ref[blocks], order_ref[blocks + 1]

    shape = (sources, marks_ref.shape[2])
    in_row = shape[1] // shard_pages
    row = g * 2 + place * blocks // in_row
    kept = jnp.zeros(shape, jnp.float32)
    for r in range(4):
        kept = jnp.where(row == r, marks_ref[:, r, :].astype(jnp.float32), kept)
    lane = lax.broadcasted_iota(jnp.int32, shape, 1)
    source = lax.broadcasted_iota(jnp.int32, shape, 0)
    first_query = starts + (place * blocks // in_row * in_row + lane // shard_pages) * tokens
    first_key = (source * blocks + z) * length + lane % shard_pages * page
    causal = jnp.clip(first_query - first_key, -2 * page, 2 * page)
    mask_ref[...] = jnp.where(kept > 0.5, causal, -2 * page)
    pltpu.sync_copy(mask_ref, reach_ref)
    here = place * blocks % in_row

    def reach_of(p, b):
        return reach_ref[p // shard_pages, (here + order_ref[b]) * shard_pages + p % shard_pages]


    def place(p, counts):
        full, some = counts
        reaches = [reach_of(p, b) for b in range(blocks)]
        low = functools.reduce(jnp.minimum, reaches)
        high = functools.reduce(jnp.maximum, reaches)
        pages_ref[full] = p
        pages_ref[masked_at + some] = p
        whole = low >= page - 1
        part = jnp.logical_and(high > -tokens, low < page - 1)
        return full + whole.astype(jnp.int32), some + part.astype(jnp.int32)

    start = (jnp.int32(0), jnp.int32(0))
    full, some = lax.fori_loop(0, all_pages, place, start, unroll=4)
    whole = full // unit

    def leftover(i, some):
        pages_ref[masked_at + some] = pages_ref[whole * unit + i]
        return some + 1

    some = lax.fori_loop(0, full - whole * unit, leftover, some)
    rounds = (some + unit - 1) // unit

    def pad(i, _):
        pages_ref[masked_at + some + i] = -1
        return 0

    lax.fori_loop(0, rounds * unit - some, pad, 0)

    ahead = lax.broadcasted_iota(jnp.int32, (tokens, page), 1) - lax.broadcasted_iota(
        jnp.int32, (tokens, page), 0
    )
    top_ref[...] = jnp.full(top_ref.shape, NEG_FILL, jnp.float32)
    sum_ref[...] = jnp.zeros(sum_ref.shape, jnp.float32)
    acc_ref[...] = jnp.zeros(acc_ref.shape, jnp.float32)

    def fetch(p, at):
        first = pl.multiple_of(at + p % shard_pages * page, page)
        return kv_ref[p // shard_pages, pl.ds(first, page), :]

    def first_pass(i, base, slot, masked):
        ps = [pages_ref[base + i * unit + u] for u in range(unit)]
        pages_at = [jnp.maximum(p, 0) for p in ps]
        k = jnp.concatenate([fetch(p, 0) for p in pages_at], axis=0)
        for b in range(blocks):
            at = pl.ds(b * rows, rows)
            s = lax.dot_general(
                queries[b][...], k, (((1,), (1,)), ((), ())), preferred_element_type=jnp.float32
            )
            top = top_ref[at, :]
            for u in range(unit):
                x = s[:, u * page : (u + 1) * page]
                if masked:
                    reach = jnp.where(ps[u] < 0, -2 * page, reach_of(pages_at[u], b))
                    x = x.reshape(per_group, tokens, page)
                    x = jnp.where((ahead <= reach)[None], x, NEG_FILL).reshape(rows, page)
                s_ref[slot, at, u * page : (u + 1) * page] = x
                top = jnp.maximum(top, x)
            top_ref[at, :] = top
        return 0

    def second_pass(i, base, slot):
        pages_at = [jnp.maximum(pages_ref[base + i * unit + u], 0) for u in range(unit)]
        v = jnp.concatenate([fetch(p, length) for p in pages_at], axis=0)
        for b in range(blocks):
            at = pl.ds(b * rows, rows)
            top = top_ref[at, :]
            weights = [
                jnp.exp2(s_ref[slot, at, u * page : (u + 1) * page] - top) for u in range(unit)
            ]
            sum_ref[at, :] = sum_ref[at, :] + functools.reduce(jnp.add, weights)
            weights = jnp.concatenate([w.astype(jnp.bfloat16) for w in weights], axis=1)
            acc_ref[at, :] = acc_ref[at, :] + jnp.dot(
                weights, v, preferred_element_type=jnp.float32
            )
        return 0

    lax.fori_loop(0, whole, lambda i, _: first_pass(i, 0, i, False), 0)
    lax.fori_loop(0, rounds, lambda i, _: first_pass(i, masked_at, whole + i, True), 0)
    for b in range(blocks):
        at = pl.ds(b * rows, rows)
        top = jnp.max(top_ref[at, :], axis=1, keepdims=True)
        top_ref[at, :] = jnp.broadcast_to(top, (rows, page))
    lax.fori_loop(0, whole, lambda i, _: second_pass(i, 0, i), 0)
    lax.fori_loop(0, rounds, lambda i, _: second_pass(i, masked_at, whole + i), 0)
    for b in range(blocks):
        at = pl.ds(b * rows, rows)
        total = jnp.sum(sum_ref[at, :], axis=1, keepdims=True)
        total = jnp.maximum(total, 1e-30)
        out = (acc_ref[at, :] / total).astype(jnp.bfloat16)
        lse = top_ref[at, :] + jnp.log2(total)
        across = [
            jnp.sum(
                jnp.where(ahead == 0, lse[h * tokens : (h + 1) * tokens], 0.0),
                axis=0,
                keepdims=True,
            )
            for h in range(per_group)
        ]
        across.append(jnp.zeros((8 - per_group, page), jnp.float32))
        across = jnp.concatenate(across, axis=0)
        high = across.astype(jnp.bfloat16).astype(jnp.float32)
        middle = (across - high).astype(jnp.bfloat16).astype(jnp.float32)
        low = across - high - middle
        tail = jnp.concatenate([high, middle, low, jnp.zeros_like(low)], axis=0)
        tail = tail.astype(jnp.bfloat16)
        packed_ref[order_ref[b], 0, pl.ds(0, rows), :] = out
        packed_ref[order_ref[b], 0, pl.ds(rows, 32), :] = tail


def attend(queries, kv, per_group, starts, order):
    held = [q.shape[0] for q in queries]
    blocks = sum(held)
    _, groups, rows, width = queries[0].shape
    sources, height, _ = kv.shape
    height = (height - 16) // groups
    page = 128
    pages = sources * (height // 2 // page)
    unit = 4
    packed = (blocks, groups, rows + 32, width)
    scores = blocks * groups * rows * pages * page // 2
    return pl.pallas_call(
        functools.partial(attend_kernel, per_group, unit, page, held, starts),
        grid_spec=pltpu.PrefetchScalarGridSpec(
            num_scalar_prefetch=1,
            grid=(groups,),
            in_specs=[pl.BlockSpec((n, 1, rows, width), lambda g, *_: (0, g, 0, 0)) for n in held]
            + [
                pl.BlockSpec((sources, height, width), lambda g, *_: (0, g, 0)),
                pl.BlockSpec((sources, 16, width), lambda g, *_: (0, groups * height // 16, 0)),
            ],
            out_specs=pl.BlockSpec((blocks, 1, rows + 32, width), lambda g, *_: (0, g, 0, 0)),
            scratch_shapes=[
                pltpu.SMEM((sources, width), jnp.int32),
                pltpu.SMEM((2 * (pages + unit),), jnp.int32),
                pltpu.VMEM((sources, width), jnp.int32),
                pltpu.VMEM((pages // unit + 1, blocks * rows, unit * page), jnp.float32),
                pltpu.VMEM((blocks * rows, page), jnp.float32),
                pltpu.VMEM((blocks * rows, page), jnp.float32),
                pltpu.VMEM((blocks * rows, width), jnp.float32),
            ],
        ),
        out_shape=jax.ShapeDtypeStruct(packed, jnp.bfloat16),
        compiler_params=pltpu.CompilerParams(vmem_limit_bytes=VMEM_LIMIT),
        cost_estimate=pl.CostEstimate(
            flops=8 * scores * width, bytes_accessed=8 * 1024 * 1024, transcendentals=scores
        ),
        name="attend",
    )(order, *queries, kv, kv)


def combine_kernel(per_group, parts_ref, table_ref, out_ref):
    sources, groups, height, width = parts_ref.shape
    rows = height - 32
    tokens = rows // per_group
    for g in range(groups):
        tails = parts_ref[:, g, pl.ds(rows, 32), :].astype(jnp.float32)
        lse = tails[:, 0:8] + tails[:, 8:16] + tails[:, 16:24]
        weights = jnp.exp2(lse - jnp.max(lse, axis=0, keepdims=True))
        weights = weights / jnp.sum(weights, axis=0, keepdims=True)
        weights = weights.reshape(sources * 8, width).T
        attended = []
        for h in range(per_group):
            one = jnp.zeros((tokens, width), jnp.float32)
            for e in range(sources):
                value = parts_ref[e, g, pl.ds(h * tokens, tokens), :].astype(jnp.float32)
                one = one + value * weights[:tokens, e * 8 + h : e * 8 + h + 1]
            attended.append(one)
        attended = jnp.concatenate(attended, axis=0)
        high = attended.astype(jnp.bfloat16)
        low = (attended - high.astype(jnp.float32)).astype(jnp.bfloat16)
        restored = jnp.dot(high, table_ref[...], preferred_element_type=jnp.float32)
        restored = restored + jnp.dot(low, table_ref[...], preferred_element_type=jnp.float32)
        restored = (restored * (1.0 / math.sqrt(width))).astype(jnp.bfloat16)
        for copy in range(out_ref.shape[0]):
            for h in range(per_group):
                at = (g * per_group + h) * width
                out_ref[copy, :, at : at + width] = restored[h * tokens : (h + 1) * tokens]


def combine(parts, table, per_group, copies):
    _, groups, height, width = parts.shape
    tokens = (height - 32) // per_group
    return pl.pallas_call(
        functools.partial(combine_kernel, per_group),
        out_shape=jax.ShapeDtypeStruct((copies, tokens, groups * per_group * width), jnp.bfloat16),
        compiler_params=pltpu.CompilerParams(vmem_limit_bytes=VMEM_LIMIT),
        name="combine",
    )(parts, table)


def project_kernel(place_ref, rows_ref, own_ref, other_ref, keep_ref, send_ref):
    _, tokens, _ = rows_ref.shape
    columns = own_ref.shape[0]
    x, x_hi, core = place_ref[0], place_ref[1], place_ref[2]
    wanted = [2 * hi + c for c in (core, 1 - core) for hi in (x_hi, 1 - x_hi)]
    rows = jnp.concatenate([rows_ref[i] for i in wanted], axis=0)
    for side, weights_ref in ((x, own_ref), (1 - x, other_ref)):
        at = pl.ds(pl.multiple_of(side * columns, columns), columns)
        terms = lax.dot_general(
            rows, weights_ref[...], (((1,), (1,)), ((), ())), preferred_element_type=jnp.float32
        ).astype(jnp.bfloat16)
        for i in range(2):
            keep_ref[i, :, at] = terms[i * tokens : (i + 1) * tokens]
            send_ref[i, :, at] = terms[(2 + i) * tokens : (3 + i) * tokens]


def project(rows, own, other, place):
    _, tokens, _ = rows.shape
    columns = own.shape[0]
    whole = pl.BlockSpec(memory_space=pltpu.VMEM)
    return pl.pallas_call(
        project_kernel,
        in_specs=[pl.BlockSpec(memory_space=pltpu.SMEM), whole, whole, whole],
        out_shape=[jax.ShapeDtypeStruct((2, tokens, 2 * columns), jnp.bfloat16)] * 2,
        compiler_params=pltpu.CompilerParams(vmem_limit_bytes=VMEM_LIMIT),
        name="project",
    )(place, rows, own, other)


def on_device(queries, cache_codes, cache_scales, pattern, out_weight):
    ny, nx, nz = (lax.axis_size(a) for a in (Y, X, Z))
    y, x, z = (lax.axis_index(a) for a in (Y, X, Z))
    x_hi, core = (lax.axis_index(a) for a in GRP)
    plane = ny * nx
    place = y * nx + x
    block_rows = queries.shape[0]
    _, groups, shard_len, width = cache_codes.shape
    heads = queries.shape[1] // width
    per_group = heads // groups
    blocks = pattern.shape[1]
    total_len = shard_len * blocks
    total_q = block_rows * blocks
    table = hadamard(width)

    def along(block, step):
        return lax.ppermute(block, Z, [(i, (i + step) % nz) for i in range(nz)])

    def across(block, step):
        return lax.ppermute(block, PLANE, [(e, e ^ step) for e in range(plane)])

    marks = pattern.reshape(-1, width)
    kv = lax.all_to_all(dequantize(cache_codes, cache_scales, marks, plane), PLANE, 0, 0)

    rotated = rotate(queries, table.astype(jnp.bfloat16), groups)
    pair = jnp.stack([rotated, along(rotated, nz // 2)])
    held = [pair, along(pair, 1), along(pair, -1)]
    held += [along(rotated, 2)[None], along(rotated, -2)[None]]
    back = [s + far for s in (0, 1, -1) for far in (0, nz // 2)] + [2, -2]
    at = (z - jnp.array(back, jnp.int32)) % nz
    order = jnp.concatenate([at, jnp.stack([place, z])]).astype(jnp.int32)

    own = lax.all_gather(passed_after(out_weight.T, *held[1:]), Z, axis=0, tiled=True)
    other = across(own, 1)

    packed = attend(held, kv, per_group, total_len - total_q, order)
    parts = lax.all_to_all(packed, Z, 0, 0)
    restored = combine(parts, table.astype(jnp.bfloat16), per_group, ny)
    restored = lax.all_to_all(restored, Y, 0, 0)
    here = jnp.stack([x, x_hi, core]).astype(jnp.int32)
    keep, send = project(restored, own, other, here)

    send = lax.ppermute(send, GRP[1], [(0, 1), (1, 0)])
    share = (keep.astype(jnp.float32) + send.astype(jnp.float32)).astype(jnp.bfloat16)
    cores = ny // 2
    where = [(a, b, c) for a in range(ny) for b in range(cores) for c in range(2)]
    mixed = jnp.zeros(share.shape[1:], jnp.float32)
    for i in range(2):
        route = [
            ((a * cores + b) * 2 + c, ((2 * (b ^ i) + c) * cores + a // 2) * 2 + a % 2)
            for a, b, c in where
        ]
        mixed = mixed + lax.ppermute(share[i], (Y,) + GRP, route).astype(jnp.float32)
    return mixed.astype(jnp.bfloat16)


def solution(mesh):
    parts = Mesh(mesh.devices.reshape(4, 2, 8, 2, 2), (Y, X, Z) + GRP)
    ctx = (Y, X, Z)
    placed = (
        P(ctx, GRP),
        P(None, GRP, ctx, None),
        P(None, GRP, None, ctx),
        P(GRP, None, ctx),
        P(GRP, ctx),
    )
    return jax.shard_map(
        on_device, mesh=parts, in_specs=placed, out_specs=P(ctx, GRP), check_vma=False
    )
```

```python
import functools
import math

import jax
import jax.numpy as jnp
from jax import lax
from jax.experimental import pallas as pl
from jax.experimental.pallas import tpu as pltpu
from jax.sharding import Mesh
from jax.sharding import PartitionSpec as P

NEG_FILL = -1e30
LOG2E = math.log2(math.e)
VMEM_LIMIT = 60 * 1024 * 1024

Y, X, Z = "y", "x_lo", "z"
PLANE = (Y, X)
GRP = ("x_hi", "core")


def hadamard(order):
    index = jnp.arange(order, dtype=jnp.int32)
    common = index[:, None] & index[None, :]
    parity = jnp.zeros((order, order), jnp.int32)
    for shift_bit in range(int(order).bit_length()):
        parity = parity ^ common >> shift_bit & 1
    return jnp.where(parity == 1, -1.0, 1.0).astype(jnp.float32)


def dequantize_kernel(codes_ref, scales_ref, *refs):
    out = refs[-1]
    kinds, _, length, width = codes_ref.shape
    parts = scales_ref.shape[2]
    for kind in range(kinds):
        scales = scales_ref[kind, 0]
        spread = jnp.concatenate(
            [
                jnp.broadcast_to(scales[i : i + 1], (width // parts, length))
                for i in range(parts)
            ],
            axis=0,
        )
        values = (codes_ref[kind, 0].astype(jnp.float32) - 7.5) * spread.T
        values = values.astype(jnp.bfloat16)
        for copy in range(out.shape[0]):
            out[copy, pl.ds(kind * length, length), :] = values
    if len(refs) == 2:
        groups, blocks, pages = refs[0].shape
        in_row = width // pages
        lane = lax.broadcasted_iota(jnp.int32, (in_row, width), 1)
        first = lax.broadcasted_iota(jnp.int32, (in_row, width), 0) * pages
        marks = []
        for g in range(groups):
            for start in range(0, blocks, in_row):
                part = refs[0][g, start : start + in_row, :].astype(jnp.float32)
                row = jnp.zeros((in_row, width), jnp.float32)
                for p in range(pages):
                    row = jnp.where(lane == first + p, part[:, p : p + 1], row)
                marks.append(jnp.sum(row, axis=0, keepdims=True))
        marks.append(jnp.zeros((16 - len(marks), width), jnp.float32))
        marks = jnp.concatenate(marks, axis=0)
        for copy in range(out.shape[0]):
            out[copy, pl.ds(kinds * length, 16), :] = marks.astype(jnp.bfloat16)


def dequantize(codes, scales, g, copies, *marks):
    kinds, _, length, width = codes.shape
    shape = (copies, kinds * length + 16 * len(marks), width)
    return pl.pallas_call(
        dequantize_kernel,
        grid=(1,),
        in_specs=[
            pl.BlockSpec((kinds, 1, length, width), lambda i: (0, g, 0, 0)),
            pl.BlockSpec((kinds, 1) + scales.shape[2:], lambda i: (0, g, 0, 0)),
        ]
        + [pl.BlockSpec(m.shape, lambda i: (0, 0, 0)) for m in marks],
        out_specs=pl.BlockSpec(shape, lambda i: (0, 0, 0)),
        out_shape=jax.ShapeDtypeStruct(shape, jnp.bfloat16),
        compiler_params=pltpu.CompilerParams(vmem_limit_bytes=VMEM_LIMIT),
        name="dequantize",
    )(codes, scales, *marks)


def tie_kernel(*refs):
    pass


def tied(block, *after):
    anywhere = pl.BlockSpec(memory_space=pl.ANY)
    return pl.pallas_call(
        tie_kernel,
        in_specs=[anywhere] * (1 + len(after)),
        out_specs=anywhere,
        out_shape=jax.ShapeDtypeStruct(block.shape, block.dtype),
        input_output_aliases={0: 0},
        name="tie",
    )(block, *after)


def pass_kernel(block_ref, *refs):
    refs[-1][...] = block_ref[...]


def passed_after(block, *after):
    anywhere = pl.BlockSpec(memory_space=pl.ANY)
    return pl.pallas_call(
        pass_kernel,
        in_specs=[pl.BlockSpec(memory_space=pltpu.VMEM)] + [anywhere] * len(after),
        out_shape=jax.ShapeDtypeStruct(block.shape, block.dtype),
        name="pass",
    )(block, *after)


def rotate_kernel(queries_ref, table_ref, out_ref):
    groups, rows, width = out_ref.shape
    tokens = queries_ref.shape[0]
    per_group = rows // tokens
    scale = LOG2E / width
    for h in range(groups * per_group):
        turned = jnp.dot(
            queries_ref[:, h * width : (h + 1) * width],
            table_ref[...],
            preferred_element_type=jnp.float32,
        )
        at = pl.ds(h % per_group * tokens, tokens)
        out_ref[h // per_group, at, :] = (turned * scale).astype(jnp.bfloat16)


def rotate(queries, table, groups):
    tokens, columns = queries.shape
    width = table.shape[0]
    rows = columns // width // groups * tokens
    return pl.pallas_call(
        rotate_kernel,
        out_shape=jax.ShapeDtypeStruct((groups, rows, width), jnp.bfloat16),
        compiler_params=pltpu.CompilerParams(vmem_limit_bytes=VMEM_LIMIT),
        name="rotate",
    )(queries, table)


def attend_kernel(per_group, units, page, held, starts, g, order_ref, *refs):
    q_from, kv_from, marks_from = refs[: len(held)], *refs[len(held) : len(held) + 2]
    packed_ref, reach_ref, mask_ref, s_ref, top_ref, acc_ref = refs[-11:-5]
    marks_ref, kv_ref, q_ref, kv_sems, q_sems = refs[-5:]
    marks_at = marks_from.shape[1] // page * page
    half = kv_ref.shape[1] // 2
    halves = [pl.ds(0, half), pl.ds(half, half)]
    marks_copy = pltpu.make_async_copy(
        marks_from.at[:, pl.ds(marks_at, 16)], marks_ref, kv_sems.at[0]
    )
    kv_copies = [
        pltpu.make_async_copy(kv_from.at[:, at], kv_ref.at[:, at], kv_sems.at[1 + i])
        for i, at in enumerate(halves)
    ]
    q_copies = [
        pltpu.make_async_copy(
            ref.at[:, g], q_ref.at[pl.ds(sum(held[:i]), held[i])], q_sems.at[i]
        )
        for i, ref in enumerate(q_from)
    ]
    for copy in (marks_copy, kv_copies[0], *q_copies, kv_copies[1]):
        copy.start()
    queries = [q_ref.at[i] for i in range(sum(held))]
    marks_copy.wait()
    blocks = len(queries)
    rows, width = queries[0].shape
    tokens = rows // per_group
    sources, height, _ = kv_ref.shape
    length = height // 2 // page * page
    shard_pages = length // page
    unit, masked_unit = units
    place, z = order_ref[blocks], order_ref[blocks + 1]

    shape = (sources, marks_ref.shape[2])
    in_row = shape[1] // shard_pages
    row = g * 2 + place * blocks // in_row
    kept = jnp.zeros(shape, jnp.float32)
    for r in range(4):
        kept = jnp.where(row == r, marks_ref[:, r, :].astype(jnp.float32), kept)
    lane = lax.broadcasted_iota(jnp.int32, shape, 1)
    source = lax.broadcasted_iota(jnp.int32, shape, 0)
    first_query = starts + (place * blocks // in_row * in_row + lane // shard_pages) * tokens
    first_key = (source * blocks + z) * length + lane % shard_pages * page
    causal = jnp.clip(first_query - first_key, -2 * page, 2 * page)
    reach = jnp.where(kept > 0.5, causal, -2 * page)
    here = place * blocks % in_row
    mine = jnp.logical_and(lane >= here * shard_pages, lane < (here + blocks) * shard_pages)
    low = jnp.where(mine, reach, 2 * page)
    high = jnp.where(mine, reach, -2 * page)
    step = shard_pages
    while step < shape[1]:
        low = jnp.minimum(low, pltpu.roll(low, step, 1))
        high = jnp.maximum(high, pltpu.roll(high, step, 1))
        step *= 2
    first_lanes = lane < shard_pages
    whole_page = jnp.logical_and(first_lanes, low >= page - 1).astype(jnp.int32)
    some_page = jnp.logical_and(first_lanes, jnp.logical_and(high > -tokens, low < page - 1))
    some_page = some_page.astype(jnp.int32)

    def counted(flags):
        before = jnp.zeros_like(flags)
        for i in range(1, shard_pages):
            before = before + jnp.where(lane >= i, pltpu.roll(flags, i, 1), 0)
        row = jnp.sum(flags, axis=1, keepdims=True)
        above = jnp.zeros_like(row)
        for i in range(sources - 1):
            above = above + jnp.where(source[:, :1] > i, row[i : i + 1], 0)
        return before + above, jnp.sum(row, axis=0, keepdims=True)

    whole_rank, whole_total = counted(whole_page)
    some_rank, some_total = counted(some_page)
    grouped = whole_total // unit * unit
    spare = whole_total - grouped
    whole_list = jnp.zeros(shape, jnp.int32)
    some_list = jnp.full(shape, 0, jnp.int32)
    for p in range(shard_pages):
        number = source * shard_pages + p + 1
        at = slice(p, p + 1)
        in_whole = jnp.logical_and(whole_page[:, at] == 1, whole_rank[:, at] < grouped)
        spared = jnp.logical_and(whole_page[:, at] == 1, whole_rank[:, at] >= grouped)
        to_whole = jnp.where(in_whole, whole_rank[:, at], -1)
        to_some = jnp.where(spared, whole_rank[:, at] - grouped, -1)
        to_some = jnp.where(some_page[:, at] == 1, spare + some_rank[:, at], to_some)
        whole_list = whole_list + jnp.where(lane == to_whole, number, 0)
        some_list = some_list + jnp.where(lane == to_some, number, 0)
    whole_list = jnp.sum(whole_list, axis=0, keepdims=True) - 1
    some_list = jnp.sum(some_list, axis=0, keepdims=True) - 1
    mask_ref[0] = reach
    counts = jnp.broadcast_to(grouped, whole_list.shape), jnp.broadcast_to(
        spare + some_total, whole_list.shape
    )
    rest = jnp.zeros((sources - 4, shape[1]), jnp.int32)
    mask_ref[1] = jnp.concatenate([whole_list, some_list, *counts, rest], axis=0)
    pltpu.sync_copy(mask_ref, reach_ref)
    whole = reach_ref[1, 2, 0] // unit
    rounds = (reach_ref[1, 3, 0] + masked_unit - 1) // masked_unit

    def reach_of(p, b):
        return reach_ref[0, p // shard_pages, (here + order_ref[b]) * shard_pages + p % shard_pages]

    ahead = lax.broadcasted_iota(jnp.int32, (tokens, page), 1) - lax.broadcasted_iota(
        jnp.int32, (tokens, page), 0
    )
    top_ref[...] = jnp.full(top_ref.shape, NEG_FILL, jnp.float32)
    acc_ref[...] = jnp.zeros(acc_ref.shape, jnp.float32)

    def fetch(p, at):
        first = pl.multiple_of(at + p % shard_pages * page, page)
        return kv_ref[p // shard_pages, pl.ds(first, page), :]

    def first_pass(i, base, plane, size, masked):
        ps = [reach_ref[1, base, i * size + u] for u in range(size)]
        pages_at = [jnp.maximum(p, 0) for p in ps]
        k = jnp.concatenate([fetch(p, 0) for p in pages_at], axis=0)
        for b in range(blocks):
            at = pl.ds(b * rows, rows)
            s = lax.dot_general(
                queries[b][...], k, (((1,), (1,)), ((), ())), preferred_element_type=jnp.float32
            )
            top = top_ref[at, :]
            for u in range(size):
                x = s[:, u * page : (u + 1) * page]
                if masked:
                    reach = jnp.where(ps[u] < 0, -2 * page, reach_of(pages_at[u], b))
                    bias = jnp.where(ahead <= reach, 0.0, -jnp.inf)
                    x = (x.reshape(per_group, tokens, page) + bias[None]).reshape(rows, page)
                s_ref[plane + i * size + u, at, :] = x
                top = jnp.maximum(top, x)
            top_ref[at, :] = top
        return 0

    def second_pass(i, base, plane, size):
        pages_at = [jnp.maximum(reach_ref[1, base, i * size + u], 0) for u in range(size)]
        v = jnp.concatenate([fetch(p, length) for p in pages_at], axis=0)
        v = jnp.concatenate([v, jnp.ones((size * page, width), jnp.bfloat16)], axis=1)
        for b in range(blocks):
            at = pl.ds(b * rows, rows)
            top = top_ref[at, :]
            weights = jnp.concatenate(
                [
                    jnp.exp2(s_ref[plane + i * size + u, at, :] - top).astype(jnp.bfloat16)
                    for u in range(size)
                ],
                axis=1,
            )
            acc_ref[at, :] = acc_ref[at, :] + jnp.dot(
                weights, v, preferred_element_type=jnp.float32
            )
        return 0

    for copy in (kv_copies[0], *q_copies):
        copy.wait()
    masked_plane = whole * unit
    lax.fori_loop(0, whole, lambda i, _: first_pass(i, 0, 0, unit, False), 0)
    lax.fori_loop(
        0, rounds, lambda i, _: first_pass(i, 1, masked_plane, masked_unit, True), 0
    )
    for b in range(blocks):
        at = pl.ds(b * rows, rows)
        top = jnp.max(top_ref[at, :], axis=1, keepdims=True)
        top_ref[at, :] = jnp.broadcast_to(top, (rows, page))
    kv_copies[1].wait()
    lax.fori_loop(0, whole, lambda i, _: second_pass(i, 0, 0, unit), 0)
    lax.fori_loop(0, rounds, lambda i, _: second_pass(i, 1, masked_plane, masked_unit), 0)
    for b in range(blocks):
        at = pl.ds(b * rows, rows)
        total = acc_ref[at, width:]
        total = jnp.maximum(total, 1e-30)
        out = (acc_ref[at, :width] / total).astype(jnp.bfloat16)
        lse = top_ref[at, :] + jnp.log2(total)
        across = [
            jnp.sum(
                jnp.where(ahead == 0, lse[h * tokens : (h + 1) * tokens], 0.0),
                axis=0,
                keepdims=True,
            )
            for h in range(per_group)
        ]
        across.append(jnp.zeros((8 - per_group, page), jnp.float32))
        across = jnp.concatenate(across, axis=0)
        high = across.astype(jnp.bfloat16).astype(jnp.float32)
        middle = (across - high).astype(jnp.bfloat16).astype(jnp.float32)
        low = across - high - middle
        tail = jnp.concatenate([high + pltpu.roll(middle, page // 2, 1), low], axis=0)
        tail = tail.astype(jnp.bfloat16)
        packed_ref[order_ref[b], 0, pl.ds(0, rows), :] = out
        packed_ref[order_ref[b], 0, pl.ds(rows, 16), :] = tail


def attend(queries, kv, marks, g, per_group, starts, order, *others):
    held = [q.shape[0] for q in queries]
    blocks = sum(held)
    _, groups, rows, width = queries[0].shape
    sources, height, _ = kv.shape
    page = 128
    height = height // page * page
    pages = sources * (height // 2 // page)
    units = (4, 2)
    packed = (blocks, groups, rows + 16, width)
    scores = blocks * rows * pages * page // 2
    return pl.pallas_call(
        functools.partial(attend_kernel, per_group, units, page, held, starts, g),
        grid_spec=pltpu.PrefetchScalarGridSpec(
            num_scalar_prefetch=1,
            grid=(1,),
            in_specs=[pl.BlockSpec(memory_space=pl.ANY)] * (len(held) + 2 + len(others)),
            out_specs=pl.BlockSpec((blocks, 1, rows + 16, width), lambda i, *_: (0, g, 0, 0)),
            scratch_shapes=[
                pltpu.SMEM((2, sources, width), jnp.int32),
                pltpu.VMEM((2, sources, width), jnp.int32),
                pltpu.VMEM((pages + units[1], blocks * rows, page), jnp.float32),
                pltpu.VMEM((blocks * rows, page), jnp.float32),
                pltpu.VMEM((blocks * rows, 2 * width), jnp.float32),
                pltpu.VMEM((sources, 16, width), jnp.bfloat16),
                pltpu.VMEM((sources, height, width), jnp.bfloat16),
                pltpu.VMEM((blocks, rows, width), jnp.bfloat16),
                pltpu.SemaphoreType.DMA((3,)),
                pltpu.SemaphoreType.DMA((len(held),)),
            ],
        ),
        out_shape=jax.ShapeDtypeStruct(packed, jnp.bfloat16),
        input_output_aliases={len(held) + 3: 0} if others else {},
        compiler_params=pltpu.CompilerParams(vmem_limit_bytes=VMEM_LIMIT),
        cost_estimate=pl.CostEstimate(
            flops=8 * scores * width, bytes_accessed=8 * 1024 * 1024, transcendentals=scores
        ),
        name="attend",
    )(order, *queries, kv, marks, *others)


def combine_kernel(per_group, parts_ref, table_ref, out_ref):
    sources, groups, height, width = parts_ref.shape
    rows = height - 16
    tokens = rows // per_group
    for g in range(groups):
        tails = parts_ref[:, g, pl.ds(rows, 16), :].astype(jnp.float32)
        middle = pltpu.roll(tails[:, 0:8].reshape(sources * 8, width), width // 2, 1)
        lse = tails[:, 0:8] + middle.reshape(sources, 8, width) + tails[:, 8:16]
        weights = jnp.exp2(lse - jnp.max(lse, axis=0, keepdims=True))
        weights = weights / jnp.sum(weights, axis=0, keepdims=True)
        weights = weights.reshape(sources * 8, width).T
        attended = []
        for h in range(per_group):
            one = jnp.zeros((tokens, width), jnp.float32)
            for e in range(sources):
                value = parts_ref[e, g, pl.ds(h * tokens, tokens), :].astype(jnp.float32)
                one = one + value * weights[:tokens, e * 8 + h : e * 8 + h + 1]
            attended.append(one)
        attended = jnp.concatenate(attended, axis=0)
        high = attended.astype(jnp.bfloat16)
        low = (attended - high.astype(jnp.float32)).astype(jnp.bfloat16)
        restored = jnp.dot(high, table_ref[...], preferred_element_type=jnp.float32)
        restored = restored + jnp.dot(low, table_ref[...], preferred_element_type=jnp.float32)
        restored = (restored * (1.0 / math.sqrt(width))).astype(jnp.bfloat16)
        for copy in range(out_ref.shape[0]):
            for h in range(per_group):
                at = (g * per_group + h) * width
                out_ref[copy, :, at : at + width] = restored[h * tokens : (h + 1) * tokens]


def combine(parts, table, per_group, copies):
    _, groups, height, width = parts.shape
    tokens = (height - 16) // per_group
    return pl.pallas_call(
        functools.partial(combine_kernel, per_group),
        out_shape=jax.ShapeDtypeStruct((copies, tokens, groups * per_group * width), jnp.bfloat16),
        compiler_params=pltpu.CompilerParams(vmem_limit_bytes=VMEM_LIMIT),
        name="combine",
    )(parts, table)


def project_kernel(place_ref, rows_ref, own_ref, other_ref, keep_ref, send_ref):
    _, tokens, _ = rows_ref.shape
    columns = own_ref.shape[0]
    x, x_hi, core = place_ref[0], place_ref[1], place_ref[2]
    wanted = [2 * hi + c for c in (core, 1 - core) for hi in (x_hi, 1 - x_hi)]
    rows = jnp.concatenate([rows_ref[i] for i in wanted], axis=0)
    for side, weights_ref in ((x, own_ref), (1 - x, other_ref)):
        at = pl.ds(pl.multiple_of(side * columns, columns), columns)
        terms = lax.dot_general(
            rows, weights_ref[...], (((1,), (1,)), ((), ())), preferred_element_type=jnp.float32
        ).astype(jnp.bfloat16)
        for i in range(2):
            keep_ref[i, :, at] = terms[i * tokens : (i + 1) * tokens]
            send_ref[i, :, at] = terms[(2 + i) * tokens : (3 + i) * tokens]


def project(rows, own, other, place):
    _, tokens, _ = rows.shape
    columns = own.shape[0]
    whole = pl.BlockSpec(memory_space=pltpu.VMEM)
    return pl.pallas_call(
        project_kernel,
        in_specs=[pl.BlockSpec(memory_space=pltpu.SMEM), whole, whole, whole],
        out_shape=[jax.ShapeDtypeStruct((2, tokens, 2 * columns), jnp.bfloat16)] * 2,
        compiler_params=pltpu.CompilerParams(vmem_limit_bytes=VMEM_LIMIT),
        name="project",
    )(place, rows, own, other)


def on_device(queries, cache_codes, cache_scales, pattern, out_weight):
    ny, nx, nz = (lax.axis_size(a) for a in (Y, X, Z))
    y, x, z = (lax.axis_index(a) for a in (Y, X, Z))
    x_hi, core = (lax.axis_index(a) for a in GRP)
    plane = ny * nx
    place = y * nx + x
    block_rows = queries.shape[0]
    _, groups, shard_len, width = cache_codes.shape
    heads = queries.shape[1] // width
    per_group = heads // groups
    blocks = pattern.shape[1]
    total_len = shard_len * blocks
    total_q = block_rows * blocks
    table = hadamard(width)

    def along(block, step):
        return lax.ppermute(block, Z, [(i, (i + step) % nz) for i in range(nz)])

    def across(block, step):
        return lax.ppermute(block, PLANE, [(e, e ^ step) for e in range(plane)])

    first = dequantize(cache_codes, cache_scales, 0, plane, pattern)
    second = dequantize(cache_codes, cache_scales, 1, plane)
    first = lax.all_to_all(first, PLANE, 0, 0)

    rotated = rotate(queries, table.astype(jnp.bfloat16), groups)
    pair = jnp.stack([rotated, along(rotated, nz // 2)])
    held = [pair, along(pair, 1), along(pair, -1)]
    held += [along(rotated, 2)[None], along(rotated, -2)[None]]
    back = [s + far for s in (0, 1, -1) for far in (0, nz // 2)] + [2, -2]
    at = (z - jnp.array(back, jnp.int32)) % nz
    second = tied(second, first[0, :16], *(h[-1, 0, :16] for h in (held[0], held[3], held[4])))
    second = lax.all_to_all(second, PLANE, 0, 0)
    order = jnp.concatenate([at, jnp.stack([place, z])]).astype(jnp.int32)

    own = lax.all_gather(passed_after(out_weight.T, *held[1:]), Z, axis=0, tiled=True)
    other = across(own, 1)

    starts = total_len - total_q
    packed = attend(held, first, first, 0, per_group, starts, order)
    packed = attend(held, second, first, 1, per_group, starts, order, packed)
    parts = lax.all_to_all(packed, Z, 0, 0)
    restored = combine(parts, table.astype(jnp.bfloat16), per_group, ny)
    restored = lax.all_to_all(restored, Y, 0, 0)
    here = jnp.stack([x, x_hi, core]).astype(jnp.int32)
    keep, send = project(restored, own, other, here)

    send = lax.ppermute(send, GRP[1], [(0, 1), (1, 0)])
    share = (keep.astype(jnp.float32) + send.astype(jnp.float32)).astype(jnp.bfloat16)
    cores = ny // 2
    where = [(a, b, c) for a in range(ny) for b in range(cores) for c in range(2)]
    mixed = jnp.zeros(share.shape[1:], jnp.float32)
    for i in range(2):
        route = [
            ((a * cores + b) * 2 + c, ((2 * (b ^ i) + c) * cores + a // 2) * 2 + a % 2)
            for a, b, c in where
        ]
        mixed = mixed + lax.ppermute(share[i], (Y,) + GRP, route).astype(jnp.float32)
    return mixed.astype(jnp.bfloat16)


def solution(mesh):
    parts = Mesh(mesh.devices.reshape(4, 2, 8, 2, 2), (Y, X, Z) + GRP)
    ctx = (Y, X, Z)
    placed = (
        P(ctx, GRP),
        P(None, GRP, ctx, None),
        P(None, GRP, None, ctx),
        P(GRP, None, ctx),
        P(GRP, ctx),
    )
    return jax.shard_map(
        on_device, mesh=parts, in_specs=placed, out_specs=P(ctx, GRP), check_vma=False
    )
```

```python
import functools
import math

import jax
import jax.numpy as jnp
from jax import lax
from jax.experimental import pallas as pl
from jax.experimental.pallas import tpu as pltpu
from jax.sharding import Mesh
from jax.sharding import PartitionSpec as P

NEG_FILL = -1e30
LOG2E = math.log2(math.e)
VMEM_LIMIT = 60 * 1024 * 1024

Y, X, Z = "y", "x_lo", "z"
PLANE = (Y, X)
GRP = ("x_hi", "core")


def hadamard(order):
    index = jnp.arange(order, dtype=jnp.int32)
    common = index[:, None] & index[None, :]
    parity = jnp.zeros((order, order), jnp.int32)
    for shift_bit in range(int(order).bit_length()):
        parity = parity ^ common >> shift_bit & 1
    return jnp.where(parity == 1, -1.0, 1.0).astype(jnp.float32)


def dequantize_kernel(codes_ref, scales_ref, pattern_ref, out):
    kinds, groups, length, width = codes_ref.shape
    parts = scales_ref.shape[2]
    for g in range(groups):
        for kind in range(kinds):
            scales = scales_ref[kind, g]
            spread = jnp.concatenate(
                [
                    jnp.broadcast_to(scales[i : i + 1], (width // parts, length))
                    for i in range(parts)
                ],
                axis=0,
            )
            values = (codes_ref[kind, g].astype(jnp.float32) - 7.5) * spread.T
            values = values.astype(jnp.bfloat16)
            for copy in range(out.shape[0]):
                out[copy, pl.ds((g * kinds + kind) * length, length), :] = values
    groups, pages, blocks = pattern_ref.shape
    in_row = width // pages
    lane = lax.broadcasted_iota(jnp.int32, (in_row, width), 1)
    first = lax.broadcasted_iota(jnp.int32, (in_row, width), 0) * pages
    marks = []
    for g in range(groups):
        kept = pattern_ref[g].astype(jnp.float32)
        kept = jnp.concatenate([kept, jnp.zeros((pages, width - blocks), jnp.float32)], axis=1)
        kept = jnp.concatenate([kept, jnp.zeros((width - pages, width), jnp.float32)], axis=0).T
        for start in range(0, blocks, in_row):
            part = kept[start : start + in_row]
            row = jnp.zeros((in_row, width), jnp.float32)
            for p in range(pages):
                row = jnp.where(lane == first + p, part[:, p : p + 1], row)
            marks.append(jnp.sum(row, axis=0, keepdims=True))
    marks.append(jnp.zeros((16 - len(marks), width), jnp.float32))
    marks = jnp.concatenate(marks, axis=0).astype(jnp.bfloat16)
    for copy in range(out.shape[0]):
        out[copy, pl.ds(kinds * groups * length, 16), :] = marks


def dequantize(codes, scales, pattern, copies):
    kinds, groups, length, width = codes.shape
    return pl.pallas_call(
        dequantize_kernel,
        out_shape=jax.ShapeDtypeStruct(
            (copies, kinds * groups * length + 16, width), jnp.bfloat16
        ),
        compiler_params=pltpu.CompilerParams(vmem_limit_bytes=VMEM_LIMIT),
        name="dequantize",
    )(codes, scales, pattern)


def pass_kernel(block_ref, *refs):
    refs[-1][...] = block_ref[...]


def passed_after(block, *after):
    anywhere = pl.BlockSpec(memory_space=pl.ANY)
    return pl.pallas_call(
        pass_kernel,
        in_specs=[pl.BlockSpec(memory_space=pltpu.VMEM)] + [anywhere] * len(after),
        out_shape=jax.ShapeDtypeStruct(block.shape, block.dtype),
        name="pass",
    )(block, *after)


def rotate_kernel(queries_ref, table_ref, out_ref):
    groups, rows, width = out_ref.shape
    tokens = queries_ref.shape[0]
    per_group = rows // tokens
    scale = LOG2E / width
    for h in range(groups * per_group):
        turned = jnp.dot(
            queries_ref[:, h * width : (h + 1) * width],
            table_ref[...],
            preferred_element_type=jnp.float32,
        )
        at = pl.ds(h % per_group * tokens, tokens)
        out_ref[h // per_group, at, :] = (turned * scale).astype(jnp.bfloat16)


def rotate(queries, table, groups):
    tokens, columns = queries.shape
    width = table.shape[0]
    rows = columns // width // groups * tokens
    return pl.pallas_call(
        rotate_kernel,
        out_shape=jax.ShapeDtypeStruct((groups, rows, width), jnp.bfloat16),
        compiler_params=pltpu.CompilerParams(vmem_limit_bytes=VMEM_LIMIT),
        name="rotate",
    )(queries, table)


def attend_kernel(per_group, units, page, held, starts, order_ref, *refs):
    q_from, kv_from, marks_from = refs[: len(held)], *refs[len(held) : len(held) + 2]
    out_ref, reach_ref, mask_ref, s_ref, top_ref, acc_ref = refs[-13:-7]
    marks_ref, kv_ref, q_ref, packed_ref, kv_sems, q_sems, out_sems = refs[-7:]
    groups = q_ref.shape[1]
    half = kv_ref.shape[1] // groups // 2
    marks_copy = pltpu.make_async_copy(
        marks_from.at[:, pl.ds(marks_from.shape[1] - 16, 16)], marks_ref, kv_sems.at[2 * groups]
    )
    q_copies = [
        pltpu.make_async_copy(ref, q_ref.at[pl.ds(sum(held[:i]), held[i])], q_sems.at[i])
        for i, ref in enumerate(q_from)
    ]

    def kv_copy(i):
        at = pl.ds(pl.multiple_of(i * half, half), half)
        return pltpu.make_async_copy(kv_from.at[:, at], kv_ref.at[:, at], kv_sems.at[i])

    def out_copy(g):
        return pltpu.make_async_copy(packed_ref.at[:, g], out_ref.at[:, g], out_sems.at[g])

    marks_copy.start()
    kv_copy(0).start()
    for copy in q_copies:
        copy.start()
    for i in range(1, 2 * groups):
        kv_copy(i).start()
    marks_copy.wait()
    blocks, _, rows, width = q_ref.shape
    tokens = rows // per_group
    sources, height, _ = kv_ref.shape
    length = half
    shard_pages = length // page
    big_unit, unit, masked_unit = units
    place, z = order_ref[blocks], order_ref[blocks + 1]

    shape = (sources, marks_ref.shape[2])
    in_row = shape[1] // shard_pages
    here = place * blocks % in_row

    def list_pages(g):
        row = g * 2 + place * blocks // in_row
        kept = jnp.zeros(shape, jnp.float32)
        for r in range(4):
            kept = jnp.where(row == r, marks_ref[:, r, :].astype(jnp.float32), kept)
        lane = lax.broadcasted_iota(jnp.int32, shape, 1)
        source = lax.broadcasted_iota(jnp.int32, shape, 0)
        first_query = starts + (place * blocks // in_row * in_row + lane // shard_pages) * tokens
        first_key = (source * blocks + z) * length + lane % shard_pages * page
        causal = jnp.clip(first_query - first_key, -2 * page, 2 * page)
        reach = jnp.where(kept > 0.5, causal, -2 * page)
        mine = jnp.logical_and(lane >= here * shard_pages, lane < (here + blocks) * shard_pages)
        low = jnp.where(mine, reach, 2 * page)
        high = jnp.where(mine, reach, -2 * page)
        step = shard_pages
        while step < shape[1]:
            low = jnp.minimum(low, pltpu.roll(low, step, 1))
            high = jnp.maximum(high, pltpu.roll(high, step, 1))
            step *= 2
        first_lanes = lane < shard_pages
        whole_page = jnp.logical_and(first_lanes, low >= page - 1).astype(jnp.int32)
        some_page = jnp.logical_and(first_lanes, jnp.logical_and(high > -tokens, low < page - 1))
        some_page = some_page.astype(jnp.int32)

        def counted(flags):
            before = jnp.zeros_like(flags)
            for i in range(1, shard_pages):
                before = before + jnp.where(lane >= i, pltpu.roll(flags, i, 1), 0)
            row = jnp.sum(flags, axis=1, keepdims=True)
            above = jnp.zeros_like(row)
            for i in range(sources - 1):
                above = above + jnp.where(source[:, :1] > i, row[i : i + 1], 0)
            return before + above, jnp.sum(row, axis=0, keepdims=True)

        whole_rank, whole_total = counted(whole_page)
        some_rank, some_total = counted(some_page)
        grouped = whole_total // unit * unit
        spare = whole_total - grouped
        whole_list = jnp.zeros(shape, jnp.int32)
        some_list = jnp.full(shape, 0, jnp.int32)
        for p in range(shard_pages):
            number = source * shard_pages + p + 1
            at = slice(p, p + 1)
            in_whole = jnp.logical_and(whole_page[:, at] == 1, whole_rank[:, at] < grouped)
            spared = jnp.logical_and(whole_page[:, at] == 1, whole_rank[:, at] >= grouped)
            to_whole = jnp.where(in_whole, whole_rank[:, at], -1)
            to_some = jnp.where(spared, whole_rank[:, at] - grouped, -1)
            to_some = jnp.where(some_page[:, at] == 1, spare + some_rank[:, at], to_some)
            whole_list = whole_list + jnp.where(lane == to_whole, number, 0)
            some_list = some_list + jnp.where(lane == to_some, number, 0)
        whole_list = jnp.sum(whole_list, axis=0, keepdims=True) - 1
        some_list = jnp.sum(some_list, axis=0, keepdims=True) - 1
        mask_ref[g, 0] = reach
        counts = jnp.broadcast_to(grouped, whole_list.shape), jnp.broadcast_to(
            spare + some_total, whole_list.shape
        )
        rest = jnp.zeros((sources - 4, shape[1]), jnp.int32)
        mask_ref[g, 1] = jnp.concatenate([whole_list, some_list, *counts, rest], axis=0)

    for g in range(groups):
        list_pages(g)
    pltpu.sync_copy(mask_ref, reach_ref)
    for copy in q_copies:
        copy.wait()

    ahead = lax.broadcasted_iota(jnp.int32, (tokens, page), 1) - lax.broadcasted_iota(
        jnp.int32, (tokens, page), 0
    )
    def one_group(g, _):
        whole = reach_ref[g, 1, 2, 0] // unit
        rounds = (reach_ref[g, 1, 3, 0] + masked_unit - 1) // masked_unit
        kv_at = g * 2 * half

        def reach_of(p, b):
            lane_at = (here + order_ref[b]) * shard_pages + p % shard_pages
            return reach_ref[g, 0, p // shard_pages, lane_at]

        top_ref[...] = jnp.full(top_ref.shape, NEG_FILL, jnp.float32)
        acc_ref[...] = jnp.zeros(acc_ref.shape, jnp.float32)

        def fetch(p, at):
            first = pl.multiple_of(kv_at + at + p % shard_pages * page, page)
            return kv_ref[p // shard_pages, pl.ds(first, page), :]

        def first_pass(i, base, start, plane, size, masked):
            ps = [reach_ref[g, 1, base, start + i * size + u] for u in range(size)]
            pages_at = [jnp.maximum(p, 0) for p in ps]
            k = jnp.concatenate([fetch(p, 0) for p in pages_at], axis=0)
            for b in range(blocks):
                at = pl.ds(b * rows, rows)
                s = lax.dot_general(
                    q_ref[b, g], k, (((1,), (1,)), ((), ())), preferred_element_type=jnp.float32
                )
                top = top_ref[at, :]
                for u in range(size):
                    x = s[:, u * page : (u + 1) * page]
                    if masked:
                        reach = jnp.where(ps[u] < 0, -2 * page, reach_of(pages_at[u], b))
                        bias = jnp.where(ahead <= reach, 0.0, -jnp.inf)
                        x = (x.reshape(per_group, tokens, page) + bias[None]).reshape(rows, page)
                    s_ref[plane + i * size + u, at, :] = x
                    top = jnp.maximum(top, x)
                top_ref[at, :] = top
            return 0

        def second_pass(i, base, start, plane, size):
            pages_at = [jnp.maximum(reach_ref[g, 1, base, start + i * size + u], 0) for u in range(size)]
            v = jnp.concatenate([fetch(p, length) for p in pages_at], axis=0)
            v = jnp.concatenate([v, jnp.ones((size * page, width), jnp.bfloat16)], axis=1)
            for b in range(blocks):
                at = pl.ds(b * rows, rows)
                top = top_ref[at, :]
                weights = jnp.concatenate(
                    [
                        jnp.exp2(s_ref[plane + i * size + u, at, :] - top).astype(jnp.bfloat16)
                        for u in range(size)
                    ],
                    axis=1,
                )
                acc_ref[at, :] = acc_ref[at, :] + jnp.dot(
                    weights, v, preferred_element_type=jnp.float32
                )
            return 0

        kv_copy(2 * g).wait()
        masked_plane = whole * unit
        big = whole * unit // big_unit
        small_at = big * big_unit
        small = whole - small_at // unit
        lax.fori_loop(0, big, lambda i, _: first_pass(i, 0, 0, 0, big_unit, False), 0)
        lax.fori_loop(
            0, small, lambda i, _: first_pass(i, 0, small_at, small_at, unit, False), 0
        )
        lax.fori_loop(
            0, rounds, lambda i, _: first_pass(i, 1, 0, masked_plane, masked_unit, True), 0
        )
        for b in range(blocks):
            at = pl.ds(b * rows, rows)
            top = jnp.max(top_ref[at, :], axis=1, keepdims=True)
            top_ref[at, :] = jnp.broadcast_to(top, (rows, page))
        kv_copy(2 * g + 1).wait()
        lax.fori_loop(0, big, lambda i, _: second_pass(i, 0, 0, 0, big_unit), 0)
        lax.fori_loop(0, small, lambda i, _: second_pass(i, 0, small_at, small_at, unit), 0)
        lax.fori_loop(0, rounds, lambda i, _: second_pass(i, 1, 0, masked_plane, masked_unit), 0)
        for b in range(blocks):
            at = pl.ds(b * rows, rows)
            total = acc_ref[at, width:]
            total = jnp.maximum(total, 1e-30)
            out = (acc_ref[at, :width] / total).astype(jnp.bfloat16)
            lse = top_ref[at, :] + jnp.log2(total)
            across = [
                jnp.sum(
                    jnp.where(ahead == 0, lse[h * tokens : (h + 1) * tokens], 0.0),
                    axis=0,
                    keepdims=True,
                )
                for h in range(per_group)
            ]
            across.append(jnp.zeros((8 - per_group, page), jnp.float32))
            across = jnp.concatenate(across, axis=0)
            high = across.astype(jnp.bfloat16).astype(jnp.float32)
            middle = (across - high).astype(jnp.bfloat16).astype(jnp.float32)
            low = across - high - middle
            tail = jnp.concatenate([high + pltpu.roll(middle, page // 2, 1), low], axis=0)
            tail = tail.astype(jnp.bfloat16)
            packed_ref[order_ref[b], g, pl.ds(0, rows), :] = out
            packed_ref[order_ref[b], g, pl.ds(rows, 16), :] = tail
        out_copy(g).start()
        return 0

    lax.fori_loop(0, groups, one_group, 0)
    for g in range(groups):
        out_copy(g).wait()


def attend(queries, kv, per_group, starts, order):
    held = [q.shape[0] for q in queries]
    blocks = sum(held)
    _, groups, rows, width = queries[0].shape
    sources, height, _ = kv.shape
    page = 128
    height = height // page * page
    pages = sources * (height // groups // 2 // page)
    units = (8, 4, 2)
    packed = (blocks, groups, rows + 16, width)
    scores = blocks * groups * rows * pages * page // 2
    anywhere = pl.BlockSpec(memory_space=pl.ANY)
    return pl.pallas_call(
        functools.partial(attend_kernel, per_group, units, page, held, starts),
        in_specs=[pl.BlockSpec(memory_space=pltpu.SMEM)] + [anywhere] * (len(held) + 2),
        out_specs=anywhere,
        scratch_shapes=[
            pltpu.SMEM((groups, 2, sources, width), jnp.int32),
            pltpu.VMEM((groups, 2, sources, width), jnp.int32),
            pltpu.VMEM((pages + units[-1], blocks * rows, page), jnp.float32),
            pltpu.VMEM((blocks * rows, page), jnp.float32),
            pltpu.VMEM((blocks * rows, 2 * width), jnp.float32),
            pltpu.VMEM((sources, 16, width), jnp.bfloat16),
            pltpu.VMEM((sources, height, width), jnp.bfloat16),
            pltpu.VMEM((blocks, groups, rows, width), jnp.bfloat16),
            pltpu.VMEM(packed, jnp.bfloat16),
            pltpu.SemaphoreType.DMA((2 * groups + 1,)),
            pltpu.SemaphoreType.DMA((len(held),)),
            pltpu.SemaphoreType.DMA((groups,)),
        ],
        out_shape=jax.ShapeDtypeStruct(packed, jnp.bfloat16),
        compiler_params=pltpu.CompilerParams(vmem_limit_bytes=VMEM_LIMIT),
        cost_estimate=pl.CostEstimate(
            flops=8 * scores * width, bytes_accessed=8 * 1024 * 1024, transcendentals=scores
        ),
        name="attend",
    )(order, *queries, kv, kv)


def combine_kernel(per_group, parts_ref, table_ref, out_ref):
    sources, groups, height, width = parts_ref.shape
    rows = height - 16
    tokens = rows // per_group
    for g in range(groups):
        tails = parts_ref[:, g, pl.ds(rows, 16), :].astype(jnp.float32)
        middle = pltpu.roll(tails[:, 0:8].reshape(sources * 8, width), width // 2, 1)
        lse = tails[:, 0:8] + middle.reshape(sources, 8, width) + tails[:, 8:16]
        weights = jnp.exp2(lse - jnp.max(lse, axis=0, keepdims=True))
        weights = weights / jnp.sum(weights, axis=0, keepdims=True)
        weights = weights.reshape(sources * 8, width).T
        attended = []
        for h in range(per_group):
            one = jnp.zeros((tokens, width), jnp.float32)
            for e in range(sources):
                value = parts_ref[e, g, pl.ds(h * tokens, tokens), :].astype(jnp.float32)
                one = one + value * weights[:tokens, e * 8 + h : e * 8 + h + 1]
            attended.append(one)
        attended = jnp.concatenate(attended, axis=0)
        high = attended.astype(jnp.bfloat16)
        low = (attended - high.astype(jnp.float32)).astype(jnp.bfloat16)
        restored = jnp.dot(high, table_ref[...], preferred_element_type=jnp.float32)
        restored = restored + jnp.dot(low, table_ref[...], preferred_element_type=jnp.float32)
        restored = (restored * (1.0 / math.sqrt(width))).astype(jnp.bfloat16)
        for copy in range(out_ref.shape[0]):
            for h in range(per_group):
                at = (g * per_group + h) * width
                out_ref[copy, :, at : at + width] = restored[h * tokens : (h + 1) * tokens]


def combine(parts, table, per_group, copies):
    _, groups, height, width = parts.shape
    tokens = (height - 16) // per_group
    return pl.pallas_call(
        functools.partial(combine_kernel, per_group),
        out_shape=jax.ShapeDtypeStruct((copies, tokens, groups * per_group * width), jnp.bfloat16),
        compiler_params=pltpu.CompilerParams(vmem_limit_bytes=VMEM_LIMIT),
        name="combine",
    )(parts, table)


def project_kernel(place_ref, rows_ref, own_ref, other_ref, keep_ref, send_ref):
    _, tokens, _ = rows_ref.shape
    columns = own_ref.shape[0]
    x, x_hi, core = place_ref[0], place_ref[1], place_ref[2]
    wanted = [2 * hi + c for c in (core, 1 - core) for hi in (x_hi, 1 - x_hi)]
    rows = jnp.concatenate([rows_ref[i] for i in wanted], axis=0)
    for side, weights_ref in ((x, own_ref), (1 - x, other_ref)):
        at = pl.ds(pl.multiple_of(side * columns, columns), columns)
        terms = lax.dot_general(
            rows, weights_ref[...], (((1,), (1,)), ((), ())), preferred_element_type=jnp.float32
        ).astype(jnp.bfloat16)
        for i in range(2):
            keep_ref[i, :, at] = terms[i * tokens : (i + 1) * tokens]
            send_ref[i, :, at] = terms[(2 + i) * tokens : (3 + i) * tokens]


def project(rows, own, other, place):
    _, tokens, _ = rows.shape
    columns = own.shape[0]
    whole = pl.BlockSpec(memory_space=pltpu.VMEM)
    return pl.pallas_call(
        project_kernel,
        in_specs=[pl.BlockSpec(memory_space=pltpu.SMEM), whole, whole, whole],
        out_shape=[jax.ShapeDtypeStruct((2, tokens, 2 * columns), jnp.bfloat16)] * 2,
        compiler_params=pltpu.CompilerParams(vmem_limit_bytes=VMEM_LIMIT),
        name="project",
    )(place, rows, own, other)


def on_device(queries, cache_codes, cache_scales, pattern, out_weight):
    ny, nx, nz = (lax.axis_size(a) for a in (Y, X, Z))
    y, x, z = (lax.axis_index(a) for a in (Y, X, Z))
    x_hi, core = (lax.axis_index(a) for a in GRP)
    plane = ny * nx
    place = y * nx + x
    block_rows = queries.shape[0]
    _, groups, shard_len, width = cache_codes.shape
    heads = queries.shape[1] // width
    per_group = heads // groups
    blocks = pattern.shape[1]
    total_len = shard_len * blocks
    total_q = block_rows * blocks
    table = hadamard(width)

    def along(block, step):
        return lax.ppermute(block, Z, [(i, (i + step) % nz) for i in range(nz)])

    def across(block, step):
        return lax.ppermute(block, PLANE, [(e, e ^ step) for e in range(plane)])

    kv = lax.all_to_all(dequantize(cache_codes, cache_scales, jnp.transpose(pattern, (0, 2, 1)), plane), PLANE, 0, 0)

    rotated = rotate(queries, table.astype(jnp.bfloat16), groups)
    pair = jnp.stack([rotated, along(rotated, nz // 2)])
    held = [pair, along(pair, 1), along(pair, -1)]
    held += [along(rotated, 2)[None], along(rotated, -2)[None]]
    back = [s + far for s in (0, 1, -1) for far in (0, nz // 2)] + [2, -2]
    at = (z - jnp.array(back, jnp.int32)) % nz
    order = jnp.concatenate([at, jnp.stack([place, z])]).astype(jnp.int32)

    own = lax.all_gather(passed_after(out_weight.T, *held[1:]), Z, axis=0, tiled=True)
    other = across(own, 1)

    packed = attend(held, kv, per_group, total_len - total_q, order)
    parts = lax.all_to_all(packed, Z, 0, 0)
    restored = combine(parts, table.astype(jnp.bfloat16), per_group, ny)
    restored = lax.all_to_all(restored, Y, 0, 0)
    here = jnp.stack([x, x_hi, core]).astype(jnp.int32)
    keep, send = project(restored, own, other, here)

    send = lax.ppermute(send, GRP[1], [(0, 1), (1, 0)])
    share = (keep.astype(jnp.float32) + send.astype(jnp.float32)).astype(jnp.bfloat16)
    cores = ny // 2
    where = [(a, b, c) for a in range(ny) for b in range(cores) for c in range(2)]
    mixed = jnp.zeros(share.shape[1:], jnp.float32)
    for i in range(2):
        route = [
            ((a * cores + b) * 2 + c, ((2 * (b ^ i) + c) * cores + a // 2) * 2 + a % 2)
            for a, b, c in where
        ]
        mixed = mixed + lax.ppermute(share[i], (Y,) + GRP, route).astype(jnp.float32)
    return mixed.astype(jnp.bfloat16)


def solution(mesh):
    parts = Mesh(mesh.devices.reshape(4, 2, 8, 2, 2), (Y, X, Z) + GRP)
    ctx = (Y, X, Z)
    placed = (
        P(ctx, GRP),
        P(None, GRP, ctx, None),
        P(None, GRP, None, ctx),
        P(GRP, None, ctx),
        P(GRP, ctx),
    )
    return jax.shard_map(
        on_device, mesh=parts, in_specs=placed, out_specs=P(ctx, GRP), check_vma=False
    )
```

```python
import functools
import math

import jax
import jax.numpy as jnp
from jax import lax
from jax.experimental import pallas as pl
from jax.experimental.pallas import tpu as pltpu
from jax.sharding import Mesh
from jax.sharding import PartitionSpec as P

NEG_FILL = -1e30
LOG2E = math.log2(math.e)
VMEM_LIMIT = 60 * 1024 * 1024

Y, X, Z = "y", "x_lo", "z"
PLANE = (Y, X)
GRP = ("x_hi", "core")


def hadamard(order):
    index = jnp.arange(order, dtype=jnp.int32)
    common = index[:, None] & index[None, :]
    parity = jnp.zeros((order, order), jnp.int32)
    for shift_bit in range(int(order).bit_length()):
        parity = parity ^ common >> shift_bit & 1
    return jnp.where(parity == 1, -1.0, 1.0).astype(jnp.float32)


def dequantize_kernel(codes_ref, scales_ref, pattern_ref, out_ref, block_ref, sems):
    kinds, groups, length, width = codes_ref.shape
    parts = scales_ref.shape[2]
    copies = out_ref.shape[0]
    started = []

    def send(section, rows):
        for i in range(copies):
            copy = pltpu.make_async_copy(
                block_ref.at[rows], out_ref.at[i, rows], sems.at[section, i]
            )
            copy.start()
            started.append(copy)

    for g in range(groups):
        for kind in range(kinds):
            scales = scales_ref[kind, g]
            spread = jnp.concatenate(
                [
                    jnp.broadcast_to(scales[i : i + 1], (width // parts, length))
                    for i in range(parts)
                ],
                axis=0,
            )
            values = (codes_ref[kind, g].astype(jnp.float32) - 7.5) * spread.T
            values = values.astype(jnp.bfloat16)
            rows = pl.ds((g * kinds + kind) * length, length)
            block_ref[rows, :] = values
            send(g * kinds + kind, rows)
    groups, pages, blocks = pattern_ref.shape
    in_row = width // pages
    lane = lax.broadcasted_iota(jnp.int32, (in_row, width), 1)
    first = lax.broadcasted_iota(jnp.int32, (in_row, width), 0) * pages
    marks = []
    for g in range(groups):
        kept = pattern_ref[g].astype(jnp.float32)
        kept = jnp.concatenate([kept, jnp.zeros((pages, width - blocks), jnp.float32)], axis=1)
        kept = jnp.concatenate([kept, jnp.zeros((width - pages, width), jnp.float32)], axis=0).T
        for start in range(0, blocks, in_row):
            part = kept[start : start + in_row]
            row = jnp.zeros((in_row, width), jnp.float32)
            for p in range(pages):
                row = jnp.where(lane == first + p, part[:, p : p + 1], row)
            marks.append(jnp.sum(row, axis=0, keepdims=True))
    marks.append(jnp.zeros((16 - len(marks), width), jnp.float32))
    marks = jnp.concatenate(marks, axis=0).astype(jnp.bfloat16)
    rows = pl.ds(kinds * groups * length, 16)
    block_ref[rows, :] = marks
    send(kinds * groups, rows)
    for copy in started:
        copy.wait()


def dequantize(codes, scales, pattern, copies):
    kinds, groups, length, width = codes.shape
    shape = (kinds * groups * length + 16, width)
    return pl.pallas_call(
        dequantize_kernel,
        in_specs=[pl.BlockSpec(memory_space=pltpu.VMEM)] * 3,
        out_specs=pl.BlockSpec(memory_space=pl.ANY),
        out_shape=jax.ShapeDtypeStruct((copies,) + shape, jnp.bfloat16),
        scratch_shapes=[
            pltpu.VMEM(shape, jnp.bfloat16),
            pltpu.SemaphoreType.DMA((kinds * groups + 1, copies)),
        ],
        compiler_params=pltpu.CompilerParams(vmem_limit_bytes=VMEM_LIMIT),
        name="dequantize",
    )(codes, scales, pattern)


def pass_kernel(block_ref, *refs):
    refs[-1][...] = block_ref[...]


def passed_after(block, *after):
    anywhere = pl.BlockSpec(memory_space=pl.ANY)
    return pl.pallas_call(
        pass_kernel,
        in_specs=[pl.BlockSpec(memory_space=pltpu.VMEM)] + [anywhere] * len(after),
        out_shape=jax.ShapeDtypeStruct(block.shape, block.dtype),
        name="pass",
    )(block, *after)


def rotate_kernel(queries_ref, table_ref, out_ref):
    groups, rows, width = out_ref.shape
    tokens = queries_ref.shape[0]
    per_group = rows // tokens
    scale = LOG2E / width
    for h in range(groups * per_group):
        turned = jnp.dot(
            queries_ref[:, h * width : (h + 1) * width],
            table_ref[...],
            preferred_element_type=jnp.float32,
        )
        at = pl.ds(h % per_group * tokens, tokens)
        out_ref[h // per_group, at, :] = (turned * scale).astype(jnp.bfloat16)


def rotate(queries, table, groups):
    tokens, columns = queries.shape
    width = table.shape[0]
    rows = columns // width // groups * tokens
    return pl.pallas_call(
        rotate_kernel,
        out_shape=jax.ShapeDtypeStruct((groups, rows, width), jnp.bfloat16),
        compiler_params=pltpu.CompilerParams(vmem_limit_bytes=VMEM_LIMIT),
        name="rotate",
    )(queries, table)


def attend_kernel(per_group, units, page, held, starts, order_ref, *refs):
    q_from, kv_from, marks_from = refs[: len(held)], *refs[len(held) : len(held) + 2]
    out_ref, reach_ref, mask_ref, s_ref, top_ref, acc_ref = refs[-13:-7]
    marks_ref, kv_ref, q_ref, packed_ref, kv_sems, q_sems, out_sems = refs[-7:]
    groups = q_ref.shape[1]
    half = kv_ref.shape[1] // groups // 2
    marks_copy = pltpu.make_async_copy(
        marks_from.at[:, pl.ds(marks_from.shape[1] - 16, 16)], marks_ref, kv_sems.at[2 * groups]
    )
    q_copies = [
        pltpu.make_async_copy(ref, q_ref.at[pl.ds(sum(held[:i]), held[i])], q_sems.at[i])
        for i, ref in enumerate(q_from)
    ]

    def kv_copy(i):
        at = pl.ds(pl.multiple_of(i * half, half), half)
        return pltpu.make_async_copy(kv_from.at[:, at], kv_ref.at[:, at], kv_sems.at[i])

    def out_copy(g):
        return pltpu.make_async_copy(packed_ref.at[:, g], out_ref.at[:, g], out_sems.at[g])

    marks_copy.start()
    kv_copy(0).start()
    for copy in q_copies:
        copy.start()
    for i in range(1, 2 * groups):
        kv_copy(i).start()
    marks_copy.wait()
    blocks, _, rows, width = q_ref.shape
    tokens = rows // per_group
    sources, height, _ = kv_ref.shape
    length = half
    shard_pages = length // page
    big_unit, unit, masked_unit = units
    place, z = order_ref[blocks], order_ref[blocks + 1]

    shape = (sources, marks_ref.shape[2])
    in_row = shape[1] // shard_pages
    here = place * blocks % in_row

    def list_pages(g):
        row = g * 2 + place * blocks // in_row
        kept = jnp.zeros(shape, jnp.float32)
        for r in range(4):
            kept = jnp.where(row == r, marks_ref[:, r, :].astype(jnp.float32), kept)
        lane = lax.broadcasted_iota(jnp.int32, shape, 1)
        source = lax.broadcasted_iota(jnp.int32, shape, 0)
        first_query = starts + (place * blocks // in_row * in_row + lane // shard_pages) * tokens
        first_key = (source * blocks + z) * length + lane % shard_pages * page
        causal = jnp.clip(first_query - first_key, -2 * page, 2 * page)
        reach = jnp.where(kept > 0.5, causal, -2 * page)
        mine = jnp.logical_and(lane >= here * shard_pages, lane < (here + blocks) * shard_pages)
        low = jnp.where(mine, reach, 2 * page)
        high = jnp.where(mine, reach, -2 * page)
        step = shard_pages
        while step < shape[1]:
            low = jnp.minimum(low, pltpu.roll(low, step, 1))
            high = jnp.maximum(high, pltpu.roll(high, step, 1))
            step *= 2
        first_lanes = lane < shard_pages
        whole_page = jnp.logical_and(first_lanes, low >= page - 1).astype(jnp.int32)
        some_page = jnp.logical_and(first_lanes, jnp.logical_and(high > -tokens, low < page - 1))
        some_page = some_page.astype(jnp.int32)

        def counted(flags):
            before = jnp.zeros_like(flags)
            for i in range(1, shard_pages):
                before = before + jnp.where(lane >= i, pltpu.roll(flags, i, 1), 0)
            row = jnp.sum(flags, axis=1, keepdims=True)
            above = jnp.zeros_like(row)
            for i in range(sources - 1):
                above = above + jnp.where(source[:, :1] > i, row[i : i + 1], 0)
            return before + above, jnp.sum(row, axis=0, keepdims=True)

        whole_rank, whole_total = counted(whole_page)
        some_rank, some_total = counted(some_page)
        grouped = whole_total // unit * unit
        spare = whole_total - grouped
        whole_list = jnp.zeros(shape, jnp.int32)
        some_list = jnp.full(shape, 0, jnp.int32)
        for p in range(shard_pages):
            number = source * shard_pages + p + 1
            at = slice(p, p + 1)
            in_whole = jnp.logical_and(whole_page[:, at] == 1, whole_rank[:, at] < grouped)
            spared = jnp.logical_and(whole_page[:, at] == 1, whole_rank[:, at] >= grouped)
            to_whole = jnp.where(in_whole, whole_rank[:, at], -1)
            to_some = jnp.where(spared, whole_rank[:, at] - grouped, -1)
            to_some = jnp.where(some_page[:, at] == 1, spare + some_rank[:, at], to_some)
            whole_list = whole_list + jnp.where(lane == to_whole, number, 0)
            some_list = some_list + jnp.where(lane == to_some, number, 0)
        whole_list = jnp.sum(whole_list, axis=0, keepdims=True) - 1
        some_list = jnp.sum(some_list, axis=0, keepdims=True) - 1
        mask_ref[g, 0] = reach
        counts = jnp.broadcast_to(grouped, whole_list.shape), jnp.broadcast_to(
            spare + some_total, whole_list.shape
        )
        rest = jnp.zeros((sources - 4, shape[1]), jnp.int32)
        mask_ref[g, 1] = jnp.concatenate([whole_list, some_list, *counts, rest], axis=0)

    for g in range(groups):
        list_pages(g)
    pltpu.sync_copy(mask_ref, reach_ref)
    for copy in q_copies:
        copy.wait()

    ahead = lax.broadcasted_iota(jnp.int32, (tokens, page), 1) - lax.broadcasted_iota(
        jnp.int32, (tokens, page), 0
    )
    def one_group(g, _):
        whole = reach_ref[g, 1, 2, 0] // unit
        rounds = (reach_ref[g, 1, 3, 0] + masked_unit - 1) // masked_unit
        kv_at = g * 2 * half

        def reach_of(p, b):
            lane_at = (here + order_ref[b]) * shard_pages + p % shard_pages
            return reach_ref[g, 0, p // shard_pages, lane_at]

        top_ref[...] = jnp.full(top_ref.shape, NEG_FILL, jnp.float32)
        acc_ref[...] = jnp.zeros(acc_ref.shape, jnp.float32)

        def fetch(p, at):
            first = pl.multiple_of(kv_at + at + p % shard_pages * page, page)
            return kv_ref[p // shard_pages, pl.ds(first, page), :]

        def first_pass(i, base, start, plane, size, masked):
            ps = [reach_ref[g, 1, base, start + i * size + u] for u in range(size)]
            pages_at = [jnp.maximum(p, 0) for p in ps]
            k = jnp.concatenate([fetch(p, 0) for p in pages_at], axis=0)
            for b in range(blocks):
                at = pl.ds(b * rows, rows)
                s = lax.dot_general(
                    q_ref[b, g], k, (((1,), (1,)), ((), ())), preferred_element_type=jnp.float32
                )
                top = top_ref[at, :]
                for u in range(size):
                    x = s[:, u * page : (u + 1) * page]
                    if masked:
                        reach = jnp.where(ps[u] < 0, -2 * page, reach_of(pages_at[u], b))
                        bias = jnp.where(ahead <= reach, 0.0, -jnp.inf)
                        x = (x.reshape(per_group, tokens, page) + bias[None]).reshape(rows, page)
                    s_ref[plane + i * size + u, at, :] = x
                    top = jnp.maximum(top, x)
                top_ref[at, :] = top
            return 0

        def second_pass(i, base, start, plane, size):
            pages_at = [jnp.maximum(reach_ref[g, 1, base, start + i * size + u], 0) for u in range(size)]
            v = jnp.concatenate([fetch(p, length) for p in pages_at], axis=0)
            v = jnp.concatenate([v, jnp.ones((size * page, width), jnp.bfloat16)], axis=1)
            for b in range(blocks):
                at = pl.ds(b * rows, rows)
                top = top_ref[at, :]
                weights = jnp.concatenate(
                    [
                        jnp.exp2(s_ref[plane + i * size + u, at, :] - top).astype(jnp.bfloat16)
                        for u in range(size)
                    ],
                    axis=1,
                )
                acc_ref[at, :] = acc_ref[at, :] + jnp.dot(
                    weights, v, preferred_element_type=jnp.float32
                )
            return 0

        kv_copy(2 * g).wait()
        masked_plane = whole * unit
        big = whole * unit // big_unit
        small_at = big * big_unit
        small = whole - small_at // unit
        lax.fori_loop(0, big, lambda i, _: first_pass(i, 0, 0, 0, big_unit, False), 0)
        lax.fori_loop(
            0, small, lambda i, _: first_pass(i, 0, small_at, small_at, unit, False), 0
        )
        lax.fori_loop(
            0, rounds, lambda i, _: first_pass(i, 1, 0, masked_plane, masked_unit, True), 0
        )
        for b in range(blocks):
            at = pl.ds(b * rows, rows)
            top = jnp.max(top_ref[at, :], axis=1, keepdims=True)
            top_ref[at, :] = jnp.broadcast_to(top, (rows, page))
        kv_copy(2 * g + 1).wait()
        lax.fori_loop(0, big, lambda i, _: second_pass(i, 0, 0, 0, big_unit), 0)
        lax.fori_loop(0, small, lambda i, _: second_pass(i, 0, small_at, small_at, unit), 0)
        lax.fori_loop(0, rounds, lambda i, _: second_pass(i, 1, 0, masked_plane, masked_unit), 0)
        for b in range(blocks):
            at = pl.ds(b * rows, rows)
            total = acc_ref[at, width:]
            total = jnp.maximum(total, 1e-30)
            out = (acc_ref[at, :width] / total).astype(jnp.bfloat16)
            lse = top_ref[at, :] + jnp.log2(total)
            across = [
                jnp.sum(
                    jnp.where(ahead == 0, lse[h * tokens : (h + 1) * tokens], 0.0),
                    axis=0,
                    keepdims=True,
                )
                for h in range(per_group)
            ]
            across.append(jnp.zeros((8 - per_group, page), jnp.float32))
            across = jnp.concatenate(across, axis=0)
            high = across.astype(jnp.bfloat16).astype(jnp.float32)
            middle = (across - high).astype(jnp.bfloat16).astype(jnp.float32)
            low = across - high - middle
            tail = jnp.concatenate([high + pltpu.roll(middle, page // 2, 1), low], axis=0)
            tail = tail.astype(jnp.bfloat16)
            packed_ref[order_ref[b], g, pl.ds(0, rows), :] = out
            packed_ref[order_ref[b], g, pl.ds(rows, 16), :] = tail
        out_copy(g).start()
        return 0

    lax.fori_loop(0, groups, one_group, 0)
    for g in range(groups):
        out_copy(g).wait()


def attend(queries, kv, per_group, starts, order):
    held = [q.shape[0] for q in queries]
    blocks = sum(held)
    _, groups, rows, width = queries[0].shape
    sources, height, _ = kv.shape
    page = 128
    height = height // page * page
    pages = sources * (height // groups // 2 // page)
    units = (8, 4, 2)
    packed = (blocks, groups, rows + 16, width)
    scores = blocks * groups * rows * pages * page // 2
    anywhere = pl.BlockSpec(memory_space=pl.ANY)
    return pl.pallas_call(
        functools.partial(attend_kernel, per_group, units, page, held, starts),
        in_specs=[pl.BlockSpec(memory_space=pltpu.SMEM)] + [anywhere] * (len(held) + 2),
        out_specs=anywhere,
        scratch_shapes=[
            pltpu.SMEM((groups, 2, sources, width), jnp.int32),
            pltpu.VMEM((groups, 2, sources, width), jnp.int32),
            pltpu.VMEM((pages + units[-1], blocks * rows, page), jnp.float32),
            pltpu.VMEM((blocks * rows, page), jnp.float32),
            pltpu.VMEM((blocks * rows, 2 * width), jnp.float32),
            pltpu.VMEM((sources, 16, width), jnp.bfloat16),
            pltpu.VMEM((sources, height, width), jnp.bfloat16),
            pltpu.VMEM((blocks, groups, rows, width), jnp.bfloat16),
            pltpu.VMEM(packed, jnp.bfloat16),
            pltpu.SemaphoreType.DMA((2 * groups + 1,)),
            pltpu.SemaphoreType.DMA((len(held),)),
            pltpu.SemaphoreType.DMA((groups,)),
        ],
        out_shape=jax.ShapeDtypeStruct(packed, jnp.bfloat16),
        compiler_params=pltpu.CompilerParams(vmem_limit_bytes=VMEM_LIMIT),
        cost_estimate=pl.CostEstimate(
            flops=8 * scores * width, bytes_accessed=8 * 1024 * 1024, transcendentals=scores
        ),
        name="attend",
    )(order, *queries, kv, kv)


def combine_kernel(per_group, parts_ref, table_ref, out_ref):
    sources, groups, height, width = parts_ref.shape
    rows = height - 16
    tokens = rows // per_group
    for g in range(groups):
        tails = parts_ref[:, g, pl.ds(rows, 16), :].astype(jnp.float32)
        middle = pltpu.roll(tails[:, 0:8].reshape(sources * 8, width), width // 2, 1)
        lse = tails[:, 0:8] + middle.reshape(sources, 8, width) + tails[:, 8:16]
        weights = jnp.exp2(lse - jnp.max(lse, axis=0, keepdims=True))
        weights = weights / jnp.sum(weights, axis=0, keepdims=True)
        weights = weights.reshape(sources * 8, width).T
        attended = []
        for h in range(per_group):
            one = jnp.zeros((tokens, width), jnp.float32)
            for e in range(sources):
                value = parts_ref[e, g, pl.ds(h * tokens, tokens), :].astype(jnp.float32)
                one = one + value * weights[:tokens, e * 8 + h : e * 8 + h + 1]
            attended.append(one)
        attended = jnp.concatenate(attended, axis=0)
        high = attended.astype(jnp.bfloat16)
        low = (attended - high.astype(jnp.float32)).astype(jnp.bfloat16)
        restored = jnp.dot(high, table_ref[...], preferred_element_type=jnp.float32)
        restored = restored + jnp.dot(low, table_ref[...], preferred_element_type=jnp.float32)
        restored = (restored * (1.0 / math.sqrt(width))).astype(jnp.bfloat16)
        for copy in range(out_ref.shape[0]):
            for h in range(per_group):
                at = (g * per_group + h) * width
                out_ref[copy, :, at : at + width] = restored[h * tokens : (h + 1) * tokens]


def combine(parts, table, per_group, copies):
    _, groups, height, width = parts.shape
    tokens = (height - 16) // per_group
    return pl.pallas_call(
        functools.partial(combine_kernel, per_group),
        out_shape=jax.ShapeDtypeStruct((copies, tokens, groups * per_group * width), jnp.bfloat16),
        compiler_params=pltpu.CompilerParams(vmem_limit_bytes=VMEM_LIMIT),
        name="combine",
    )(parts, table)


def project_kernel(place_ref, rows_ref, own_ref, other_ref, keep_ref, send_ref):
    _, tokens, _ = rows_ref.shape
    columns = own_ref.shape[0]
    x, x_hi, core = place_ref[0], place_ref[1], place_ref[2]
    wanted = [2 * hi + c for c in (core, 1 - core) for hi in (x_hi, 1 - x_hi)]
    rows = jnp.concatenate([rows_ref[i] for i in wanted], axis=0)
    for side, weights_ref in ((x, own_ref), (1 - x, other_ref)):
        at = pl.ds(pl.multiple_of(side * columns, columns), columns)
        terms = lax.dot_general(
            rows, weights_ref[...], (((1,), (1,)), ((), ())), preferred_element_type=jnp.float32
        ).astype(jnp.bfloat16)
        for i in range(2):
            keep_ref[i, :, at] = terms[i * tokens : (i + 1) * tokens]
            send_ref[i, :, at] = terms[(2 + i) * tokens : (3 + i) * tokens]


def project(rows, own, other, place):
    _, tokens, _ = rows.shape
    columns = own.shape[0]
    whole = pl.BlockSpec(memory_space=pltpu.VMEM)
    return pl.pallas_call(
        project_kernel,
        in_specs=[pl.BlockSpec(memory_space=pltpu.SMEM), whole, whole, whole],
        out_shape=[jax.ShapeDtypeStruct((2, tokens, 2 * columns), jnp.bfloat16)] * 2,
        compiler_params=pltpu.CompilerParams(vmem_limit_bytes=VMEM_LIMIT),
        name="project",
    )(place, rows, own, other)


def on_device(queries, cache_codes, cache_scales, pattern, out_weight):
    ny, nx, nz = (lax.axis_size(a) for a in (Y, X, Z))
    y, x, z = (lax.axis_index(a) for a in (Y, X, Z))
    x_hi, core = (lax.axis_index(a) for a in GRP)
    plane = ny * nx
    place = y * nx + x
    block_rows = queries.shape[0]
    _, groups, shard_len, width = cache_codes.shape
    heads = queries.shape[1] // width
    per_group = heads // groups
    blocks = pattern.shape[1]
    total_len = shard_len * blocks
    total_q = block_rows * blocks
    table = hadamard(width)

    def along(block, step):
        return lax.ppermute(block, Z, [(i, (i + step) % nz) for i in range(nz)])

    def across(block, step):
        return lax.ppermute(block, PLANE, [(e, e ^ step) for e in range(plane)])

    kv = lax.all_to_all(dequantize(cache_codes, cache_scales, jnp.transpose(pattern, (0, 2, 1)), plane), PLANE, 0, 0)

    rotated = rotate(queries, table.astype(jnp.bfloat16), groups)
    pair = jnp.stack([rotated, along(rotated, nz // 2)])
    held = [pair, along(pair, 1), along(pair, -1)]
    held += [along(rotated, 2)[None], along(rotated, -2)[None]]
    back = [s + far for s in (0, 1, -1) for far in (0, nz // 2)] + [2, -2]
    at = (z - jnp.array(back, jnp.int32)) % nz
    order = jnp.concatenate([at, jnp.stack([place, z])]).astype(jnp.int32)

    own = lax.all_gather(passed_after(out_weight.T, *held[1:]), Z, axis=0, tiled=True)
    other = across(own, 1)

    packed = attend(held, kv, per_group, total_len - total_q, order)
    parts = lax.all_to_all(packed, Z, 0, 0)
    restored = combine(parts, table.astype(jnp.bfloat16), per_group, ny)
    restored = lax.all_to_all(restored, Y, 0, 0)
    here = jnp.stack([x, x_hi, core]).astype(jnp.int32)
    keep, send = project(restored, own, other, here)

    send = lax.ppermute(send, GRP[1], [(0, 1), (1, 0)])
    share = (keep.astype(jnp.float32) + send.astype(jnp.float32)).astype(jnp.bfloat16)
    cores = ny // 2
    where = [(a, b, c) for a in range(ny) for b in range(cores) for c in range(2)]
    mixed = jnp.zeros(share.shape[1:], jnp.float32)
    for i in range(2):
        route = [
            ((a * cores + b) * 2 + c, ((2 * (b ^ i) + c) * cores + a // 2) * 2 + a % 2)
            for a, b, c in where
        ]
        mixed = mixed + lax.ppermute(share[i], (Y,) + GRP, route).astype(jnp.float32)
    return mixed.astype(jnp.bfloat16)


def solution(mesh):
    parts = Mesh(mesh.devices.reshape(4, 2, 8, 2, 2), (Y, X, Z) + GRP)
    ctx = (Y, X, Z)
    placed = (
        P(ctx, GRP),
        P(None, GRP, ctx, None),
        P(None, GRP, None, ctx),
        P(GRP, None, ctx),
        P(GRP, ctx),
    )
    return jax.shard_map(
        on_device, mesh=parts, in_specs=placed, out_specs=P(ctx, GRP), check_vma=False
    )
```
